32 devices in a mesh: dp: 4 (over z), row: 4 (over x, core), col: 2 (over y).
Axes of the slice: x: 2, y: 2, z: 4, core: 2. Of those that a mesh axis runs over, the one named last changes fastest.
Arguments:
- hidden_in: bfloat16 [8192, 1536], P(('dp', 'row', 'col')), may hold values from -6 to 6
- lengths: int32 [16], replicated, may hold values from 1 to 1024, as said below
- perm: int32 [16], P('dp'), may hold values from 0 to 15, as said below
- norm_gain: float32 [1536], replicated, may hold values from 0.5 to 1.5
- w_z: float32 [1536, 3072], P('dp', ('row', 'col')), may hold values from -0.15625 to 0.15625
- w_x: float32 [1536, 3072], P('dp', ('row', 'col')), may hold values from -0.15625 to 0.15625
- w_dt: float32 [1536, 48], P('dp', ('row', 'col')), may hold values from -0.15625 to 0.15625
- w_bc: float32 [1536, 256], P('dp'), may hold values from -0.15625 to 0.15625
- conv_x: float32 [4, 3072], replicated, may hold values from -3 to 3
- conv_x_bias: float32 [3072], replicated, may hold values from -3 to 3
- conv_bc: float32 [4, 256], replicated, may hold values from -3 to 3
- conv_bc_bias: float32 [256], replicated, may hold values from -3 to 3
- dt_bias: float32 [48], replicated, may hold values from -7 to -3
- a_log: float32 [48], replicated, may hold values from 0 to 2.77
- skip_d: float32 [48], replicated, may hold values from 0.5 to 1.5
- gate_gain: float32 [3072], replicated, may hold values from 0.5 to 1.5
- w_out: float32 [3072, 1536], P(('row', 'col'), 'dp'), may hold values from -0.109375 to 0.109375
- grad_out: bfloat16 [8192, 1536], P(('dp', 'row', 'col')), may hold values from -6 to 6
Outputs:
- block_out: bfloat16 [8192, 1536], P(('dp', 'row', 'col'))
- grad_in: bfloat16 [8192, 1536], P(('dp', 'row', 'col'))
- g_norm_gain: float32 [1536], replicated
- g_w_z: float32 [1536, 3072], P('dp', ('row', 'col'))
- g_w_x: float32 [1536, 3072], P('dp', ('row', 'col'))
- g_w_dt: float32 [1536, 48], P('dp', ('row', 'col'))
- g_w_bc: float32 [1536, 256], P('dp')
- g_conv_x: float32 [4, 3072], replicated
- g_conv_x_bias: float32 [3072], replicated
- g_conv_bc: float32 [4, 256], replicated
- g_conv_bc_bias: float32 [256], replicated
- g_dt_bias: float32 [48], replicated
- g_a_log: float32 [48], replicated
- g_skip_d: float32 [48], replicated
- g_gate_gain: float32 [3072], replicated
- g_w_out: float32 [3072, 1536], P(('row', 'col'), 'dp')
The draws below stay inside these ranges and needn't reach their ends.
Inputs may be any that keep to these rules, and one draw needn't show every extreme that they name: In every group the 4 lengths of its slots sum to 2048, and the longest of them is exactly 1024. `perm`: A permutation of the sequences.
All inputs are finite; a program needn't handle non-finite values.
Results may differ from the reference program's by a relative error of at most 0.012.
Values may be sent and summed in bfloat16 or wider, within the bound.
A program may use at most 192 MiB of HBM per device.

```python
from functools import partial
import jax
import jax.numpy as jnp
from jax import lax

D = 1536
HEADS = 48
STATE = 128
KERNEL = 4
SPAN = 256
SPG = 4
TOK_GRP = 2048
INNER = 3072
SEQS = 16
TOKENS = 8192
N_DP = 4


def deal_sequences(key):
    key_first, key_second, key_layout, key_order = jax.random.split(key, 4)
    half_len = TOK_GRP // 2
    first_len = jax.random.randint(key_first, (N_DP,), 1, half_len - 1)
    second_len = jax.random.randint(key_second, (N_DP,), jnp.ones((N_DP,), jnp.int32), half_len - first_len)
    third_len = half_len - first_len - second_len
    layout_pick = jax.random.randint(key_layout, (N_DP,), 0, 2)
    long_len = jnp.full((N_DP,), half_len, jnp.int32)
    layout_one = jnp.stack([first_len, long_len, second_len, third_len], axis=1)
    layout_two = jnp.stack([first_len, second_len, long_len, third_len], axis=1)
    dealt_len = jnp.where((layout_pick == 0)[:, None], layout_one, layout_two).reshape(SEQS).astype(jnp.int32)
    order = jax.random.permutation(key_order, SEQS).astype(jnp.int32)
    return (order, dealt_len)


def draw_lengths(key, part):
    order, dealt_len = deal_sequences(key)
    return jnp.zeros((SEQS,), jnp.int32).at[order].set(dealt_len)


def draw_perm(key, part):
    order, dealt_len = deal_sequences(key)
    return order


def shard_levels(key, extent, shards, low, high):
    def one(dim, shards_of):
        heights = jax.random.uniform(jax.random.fold_in(jax.random.fold_in(key, 6), dim), (shards_of,), jnp.float32, low / len(shards), high / len(shards))
        return jnp.repeat(jnp.exp(heights), extent[dim] // shards_of).reshape((-1,) + (1,) * (len(extent) - dim - 1))

    gain = one(*shards[0])
    for cut in shards[1:]:
        gain = gain * one(*cut)
    return gain


def noise(own_key, shape, spread, bound, cuts=(), kind=jnp.bfloat16):
    level = shard_levels(own_key, shape, cuts, -0.22, 0.18) if cuts else 1.0
    array = jax.random.normal(own_key, shape, jnp.float32) * spread * level
    return jnp.minimum(jnp.maximum(array, -bound), bound).astype(kind)


def setup_inputs(seed: int = 0) -> dict:
    splits = jax.random.split(jax.random.key(seed), 19)
    return {
        "hidden_in": noise(splits[0], (TOKENS, D), 1.0, 6.0, ((0, 32),)),
        "lengths": draw_lengths(jax.random.fold_in(splits[18], 71), 0),
        "perm": draw_perm(jax.random.fold_in(splits[18], 71), 0),
        "norm_gain": jnp.clip(1.0 + 0.1 * jax.random.normal(splits[3], (D,), jnp.float32), 0.5, 1.5),
        "w_z": noise(splits[4], (D, INNER), D ** -0.5, 0.15625, ((0, 4), (1, 8)), jnp.float32),
        "w_x": noise(splits[5], (D, INNER), D ** -0.5, 0.15625, ((0, 4), (1, 8)), jnp.float32),
        "w_dt": noise(splits[6], (D, HEADS), D ** -0.5, 0.15625, ((0, 4), (1, 8)), jnp.float32),
        "w_bc": noise(splits[7], (D, 2 * STATE), D ** -0.5, 0.15625, ((0, 4),), jnp.float32),
        "conv_x": noise(splits[8], (KERNEL, INNER), KERNEL ** -0.5, 3.0, (), jnp.float32),
        "conv_x_bias": noise(splits[9], (INNER,), 0.5, 3.0, (), jnp.float32),
        "conv_bc": noise(splits[10], (KERNEL, 2 * STATE), KERNEL ** -0.5, 3.0, (), jnp.float32),
        "conv_bc_bias": noise(splits[11], (2 * STATE,), 0.5, 3.0, (), jnp.float32),
        "dt_bias": jnp.clip(jax.random.uniform(splits[12], (HEADS,), jnp.float32, -7.0, -3.0), -7.0, -3.0),
        "a_log": jnp.clip(jax.random.uniform(splits[13], (HEADS,), jnp.float32, 0.0, 2.77), 0.0, 2.77),
        "skip_d": jnp.clip(jax.random.uniform(splits[14], (HEADS,), jnp.float32, 0.5, 1.5), 0.5, 1.5),
        "gate_gain": jnp.clip(1.0 + 0.1 * jax.random.normal(splits[15], (INNER,), jnp.float32), 0.5, 1.5),
        "w_out": noise(splits[16], (INNER, D), INNER ** -0.5, 0.109375, ((0, 8), (1, 4)), jnp.float32),
        "grad_out": noise(splits[17], (TOKENS, D), 1.0, 6.0, ((0, 32),)),
    }


EPSILON = 1e-05
HIGHEST = lax.Precision.HIGHEST

@jax.custom_vjp
def low(v):
    return lax.optimization_barrier(v.astype(jnp.bfloat16)).astype(jnp.float32)

@jax.custom_vjp
def low_back(v):
    return v

def low_keep(v):
    return (low(v), None)

def low_pass(kept, grad):
    return (grad,)

def back_keep(v):
    return (v, None)

def back_low(kept, grad):
    return (low(grad),)
low.defvjp(low_keep, low_pass)
low_back.defvjp(back_keep, back_low)

def norm_in(inputs, gains):
    return inputs * lax.rsqrt(lax.optimization_barrier(jnp.mean(inputs * inputs, axis=-1, keepdims=True)) + EPSILON) * gains

def dealt_lengths(lengths, slot_ids):
    seq_ids = jnp.arange(lengths.shape[0], dtype=jnp.int32)
    return lax.optimization_barrier(jnp.sum(jnp.where(slot_ids[:, None] == seq_ids[None, :], lengths[None, :], 0), axis=1)).astype(jnp.int32)

def token_layout(dealt_len, length):
    offsets = (jnp.cumsum(dealt_len) - dealt_len).astype(jnp.int32)
    positions = jnp.arange(length, dtype=jnp.int32)
    starts = lax.optimization_barrier(jnp.sum((positions[:, None] == offsets[None, :]).astype(jnp.int32), axis=1)).astype(jnp.int32)
    begin_at = lax.optimization_barrier(jnp.max(jnp.where(offsets[None, :] <= positions[:, None], offsets[None, :], 0), axis=1)).astype(jnp.int32)
    return (starts, (positions - begin_at).astype(jnp.int32))

def causal_conv(values, kernel, offset, places):
    n_taps = kernel.shape[0]
    result = kernel[n_taps - 1] * values + offset
    for back_by in range(1, n_taps):
        shifted = jnp.concatenate([jnp.zeros((back_by, values.shape[1]), values.dtype), values[:-back_by]], axis=0)
        result = result + kernel[n_taps - 1 - back_by] * jnp.where((places >= back_by)[:, None], shifted, 0.0)
    return result

def ssd_scan(x_heads, dt_soft, decay_rate, b_mat, c_mat, starts):
    length, n_heads, head_dim = x_heads.shape
    n_state = b_mat.shape[1]
    n_blocks = length // SPAN
    blocks = (x_heads.reshape(n_blocks, SPAN, n_heads, head_dim), dt_soft.reshape(n_blocks, SPAN, n_heads), b_mat.reshape(n_blocks, SPAN, n_state), c_mat.reshape(n_blocks, SPAN, n_state), starts.reshape(n_blocks, SPAN))
    positions = jnp.arange(SPAN, dtype=jnp.int32)
    lower_mask = positions[:, None] >= positions[None, :]

    def advance(hidden, block_data):
        x_block, dt_block, b_block, c_block, f_block = block_data
        log_decay = jnp.cumsum(dt_block * decay_rate[None, :], axis=0)
        segment = jnp.cumsum(f_block).astype(jnp.int32)
        same_seq = (segment[:, None] == segment[None, :]) & lower_mask
        decays = jnp.exp(jnp.where(same_seq[:, :, None], log_decay[:, None, :] - log_decay[None, :, :], -1e+30))
        gram_mat = jnp.dot(c_block, b_block.T, precision=HIGHEST)
        mixing = decays * gram_mat[:, :, None] * dt_block[None, :, :]
        inside = jnp.einsum('ijh,jhp->ihp', mixing, x_block, precision=HIGHEST)
        carried = jnp.einsum('in,hpn->ihp', c_block, hidden, precision=HIGHEST) * jnp.exp(log_decay)[:, :, None]
        carried = jnp.where((segment == 0)[:, None, None], carried, 0.0)
        last_mark = segment[-1]
        end_weight = jnp.where((segment == last_mark)[:, None], jnp.exp(log_decay[-1][None, :] - log_decay), 0.0) * dt_block
        fresh_state = jnp.einsum('jh,jhp,jn->hpn', end_weight, x_block, b_block, precision=HIGHEST)
        kept_share = jnp.where(last_mark == 0, jnp.exp(log_decay[-1]), 0.0)
        return (fresh_state + kept_share[:, None, None] * hidden, inside + carried)
    zero_state = jnp.zeros((n_heads, head_dim, n_state), x_heads.dtype)
    _, outputs = lax.scan(jax.checkpoint(advance), zero_state, blocks)
    return outputs.reshape(length, n_heads, head_dim)

def mixer(z_raw, x_raw, dt_raw, bc_raw, conv_x, conv_x_bias, conv_bc, conv_bc_bias, dt_bias, a_log, skip_d, starts, places):
    n_heads = dt_bias.shape[0]
    n_state = bc_raw.shape[1] // 2
    length = x_raw.shape[0]
    x_conv = jax.nn.silu(causal_conv(x_raw, conv_x, conv_x_bias, places))
    bc_conv = jax.nn.silu(causal_conv(bc_raw, conv_bc, conv_bc_bias, places))
    dt_soft = jax.nn.softplus(dt_raw + dt_bias)
    x_heads = x_conv.reshape(length, n_heads, -1)
    scanned = ssd_scan(x_heads, dt_soft, -jnp.exp(a_log), bc_conv[:, :n_state], bc_conv[:, n_state:], starts)
    outputs = scanned + skip_d[None, :, None] * x_heads
    return outputs.reshape(length, -1) * jax.nn.silu(z_raw)

def forward(starts, places, inputs, norm_gain, w_z, w_x, w_dt, w_bc, conv_x, conv_x_bias, conv_bc, conv_bc_bias, dt_bias, a_log, skip_d, gate_gain, w_out):
    normed = low(norm_in(inputs, norm_gain))
    z_raw = low_back(jnp.dot(normed, low(w_z), precision=HIGHEST))
    x_raw = low_back(jnp.dot(normed, low(w_x), precision=HIGHEST))
    dt_raw = low_back(jnp.dot(normed, low(w_dt), precision=HIGHEST))
    bc_raw = low_back(jnp.dot(normed, low(w_bc), precision=HIGHEST))
    gated_rows = mixer(z_raw, x_raw, dt_raw, bc_raw, conv_x, conv_x_bias, conv_bc, conv_bc_bias, dt_bias, a_log, skip_d, starts, places)
    row_scale = lax.rsqrt(lax.optimization_barrier(jnp.mean(gated_rows * gated_rows, axis=-1, keepdims=True)) + EPSILON)
    normed_out = low(gated_rows * row_scale * gate_gain)
    return inputs + jnp.dot(normed_out, low(w_out), precision=HIGHEST)

def reference(hidden_in, lengths, perm, norm_gain, w_z, w_x, w_dt, w_bc, conv_x, conv_x_bias, conv_bc, conv_bc_bias, dt_bias, a_log, skip_d, gate_gain, w_out, grad_out):
    groups_in = hidden_in.astype(jnp.float32).reshape(N_DP, TOK_GRP, D)
    groups_back = grad_out.astype(jnp.float32).reshape(N_DP, TOK_GRP, D)
    slots_all = perm.reshape(N_DP, SPG)
    params = (norm_gain, w_z, w_x, w_dt, w_bc, conv_x, conv_x_bias, conv_bc, conv_bc_bias, dt_bias, a_log, skip_d, gate_gain, w_out)

    def one_group(totals, group_data):
        inputs, cotangent, slot_ids = group_data
        starts, places = token_layout(dealt_lengths(lengths, slot_ids), TOK_GRP)
        result, pullback = jax.vjp(partial(forward, starts, places), inputs, *params)
        gradients = pullback(cotangent)
        totals = jax.tree.map(jnp.add, totals, tuple(gradients[1:]))
        return (totals, (result.astype(jnp.bfloat16), gradients[0].astype(jnp.bfloat16)))
    zero_sums = jax.tree.map(jnp.zeros_like, params)
    totals, (outputs, input_grads) = lax.scan(one_group, zero_sums, (groups_in, groups_back, slots_all))
    return (outputs.reshape(TOKENS, D), input_grads.reshape(TOKENS, D), totals[0], totals[1], totals[2], totals[3], totals[4], totals[5], totals[6], totals[7], totals[8], totals[9], totals[10], totals[11], totals[12], totals[13])
```

```python
import functools
import types

import jax
import jax.numpy as jnp
from jax import lax
from jax.experimental import pallas as pl
from jax.experimental.pallas import tpu as pltpu
from jax.sharding import PartitionSpec as P

SPAN = 256
HALF = SPAN // 2
STATE = 128
BC = 2 * STATE
KERNEL = 4
EPS = 1e-5
f32, bf16 = jnp.float32, jnp.bfloat16
MESH = pl.DeviceIdType.MESH


def nt(a, b):
    return lax.dot_general(a, b, (((1,), (1,)), ((), ())), preferred_element_type=f32)


def nn(a, b):
    return lax.dot_general(a, b, (((1,), (0,)), ((), ())), preferred_element_type=f32)


def tn(a, b):
    return lax.dot_general(a, b, (((0,), (0,)), ((), ())), preferred_element_type=f32)


def aligned(start, size):
    return pl.ds(pl.multiple_of(start, size), size)


def softplus(v):
    return jnp.maximum(v, 0.0) + jnp.log1p(jnp.exp(-jnp.abs(v)))


def split3(v):
    a = v.astype(bf16)
    w = v - a.astype(f32)
    b = w.astype(bf16)
    return jnp.concatenate([a, b, (w - b.astype(f32)).astype(bf16)], axis=0)


def merge3(v):
    return v[0:8] + v[8:16] + v[16:24]


def tri_low():
    i = lax.broadcasted_iota(jnp.int32, (SPAN, SPAN), 0)
    j = lax.broadcasted_iota(jnp.int32, (SPAN, SPAN), 1)
    return (i >= j).astype(bf16)


def decay_terms(b, offs, da):
    first = b * SPAN
    row = first + lax.broadcasted_iota(jnp.int32, (1, SPAN), 1)
    col = first + lax.broadcasted_iota(jnp.int32, (SPAN, 1), 0)

    def begin(pos):
        at = jnp.zeros_like(pos)
        for o in offs[1:]:
            at = jnp.where(pos >= o, o, at)
        return at

    beg_r, beg_c = begin(row), begin(col)
    l_row = merge3(nt(split3(da), tri_low()))
    l_col = l_row.T
    last = l_row[:, SPAN - 1 : SPAN]
    end_b = jnp.max(beg_r, axis=1, keepdims=True)
    e = jnp.where(beg_r < first, jnp.exp(l_row), 0.0)
    we = jnp.where(beg_r == end_b, jnp.exp(last - l_row), 0.0)
    kept = jnp.where(end_b < first, jnp.exp(last), 0.0)
    mask = jnp.where((beg_r == beg_c) & (row <= col), 1.0, 0.0)
    return l_row, l_col, e, we, kept, mask, row - beg_r


def wide(ref, k, rows):
    w = ref[k, rows, :]
    return jnp.concatenate([w, w], axis=1)


def fold(v):
    return v[:, 0:128] + v[:, 128:256]


def conv_forward(cur, tail, pref, rows, places):
    win = jnp.concatenate([tail, cur], axis=1)
    u = wide(pref, 3, rows) * cur + wide(pref, 4, rows)
    for s in (1, 2, 3):
        back = jnp.where(places >= s, pltpu.roll(win, s, 1)[:, 128:], 0.0)
        u = u + wide(pref, 3 - s, rows) * back
    return u


def conv_backward(R, raw, du, pref, acc, head, rows, base, tok, m):
    out = wide(pref, 3, rows) * du
    acc[4, rows, :] += fold(du)
    acc[3, rows, :] += fold(du * raw)
    for s in (1, 2, 3):
        w = du * m[s]
        win = jnp.concatenate([w, head[s - 1, rows, :]], axis=1)
        sh = pltpu.roll(win, SPAN + 128 - s, 1)[:, 0:SPAN]
        head[s - 1, rows, :] = w[:, 0:128]
        out = out + wide(pref, 3 - s, rows) * sh
        acc[3 - s, rows, :] += fold(sh * raw)
    R.dcat[base + rows.start : base + rows.stop, tok] = out.astype(bf16)


def fwd_block(b, R, offs, C, H):
    p = C // H
    tok = aligned(b * SPAN, SPAN)
    R.pr[...] = nt(R.wcat[...], R.hn[tok, :])
    R.z[:, tok] = R.pr[0:C, :].astype(bf16)
    R.xr[:, tok] = R.pr[C : 2 * C, :].astype(bf16)
    R.bcr[:, tok] = R.pr[2 * C : 2 * C + BC, :].astype(bf16)
    dr = R.pr[2 * C + BC : 2 * C + BC + 8, :] + R.ph[:, 0:1]
    R.dr[:, tok] = dr
    dt = softplus(dr)
    l_row, l_col, e, we, kept, mask, places = decay_terms(b, offs, dt * R.ph[:, 1:2])
    bcr = R.pr[2 * C : 2 * C + BC, :]
    u = conv_forward(bcr, R.tail_bc[...], R.pbc, slice(0, BC), places).astype(bf16)
    R.tail_bc[...] = bcr[:, 128:]
    R.ubc[:, tok] = u
    u = u.astype(f32)
    bc = (u * jax.nn.sigmoid(u)).astype(bf16)
    bt, ct = bc[0:STATE, :], bc[STATE:BC, :]
    R.gm[...] = tn(ct, bt) * mask
    sq = jnp.zeros((1, SPAN), f32)
    for h in range(H):
        rows = slice(h * p, (h + 1) * p)
        hh = slice(h, h + 1)
        xr = R.pr[C + h * p : C + (h + 1) * p, :]
        u = conv_forward(xr, R.tail_x[rows, :], R.px, rows, places).astype(bf16)
        R.tail_x[rows, :] = xr[:, 128:]
        R.ux[rows, tok] = u
        u = u.astype(f32)
        x = u * jax.nn.sigmoid(u)
        xd = x * dt[hh, :]
        d = jnp.exp(jnp.minimum(l_col[:, hh] - l_row[hh, :], 0.0))
        mix = (d * R.gm[...]).astype(bf16)
        st = R.state[rows, :]
        stb = st.astype(bf16)
        R.states[b, rows, :] = stb
        y = nt(xd.astype(bf16), mix) + nn(stb, ct) * e[hh, :]
        R.y[rows, tok] = y
        R.state[rows, :] = kept[hh, :] * st + nt((xd * we[hh, :]).astype(bf16), bt)
        zz = R.z[rows, tok].astype(f32)
        gy = (y + wide(R.px, 6, rows) * x) * (zz * jax.nn.sigmoid(zz))
        sq = sq + jnp.sum(gy * gy, axis=0, keepdims=True)
        R.gg[rows, tok] = (gy * wide(R.px, 5, rows)).astype(bf16)
    R.sums[pl.ds(b, 1), :] = sq


def bwd_block(b, R, offs, C, H, inner):
    p = C // H
    nb = R.sums.shape[0] // 2
    tok = aligned(b * SPAN, SPAN)
    v = R.dr[:, tok]
    dt = softplus(v)
    rate = R.ph[:, 1:2]
    l_row, l_col, e, we, kept, mask, places = decay_terms(b, offs, dt * rate)
    ubc = R.ubc[:, tok].astype(f32)
    sg = jax.nn.sigmoid(ubc)
    bc = (ubc * sg).astype(bf16)
    bt, ct = bc[0:STATE, :], bc[STATE:BC, :]
    R.gm[...] = tn(ct, bt) * mask
    r = lax.rsqrt(R.tot[pl.ds(b, 1), :] / inner + EPS)
    rs = r * r * r * R.tot[pl.ds(nb + b, 1), :] / inner
    m = [None] + [jnp.where(places >= s, 1.0, 0.0) for s in (1, 2, 3)]
    decays, directs, ends = [], [], []
    for h in range(H):
        rows = slice(h * p, (h + 1) * p)
        hh = slice(h, h + 1)
        u = R.ux[rows, tok].astype(f32)
        sx = jax.nn.sigmoid(u)
        x = u * sx
        y = R.y[rows, tok]
        zz = R.z[rows, tok].astype(f32)
        sz = jax.nn.sigmoid(zz)
        gate = zz * sz
        skip = wide(R.px, 6, rows)
        yf = y + skip * x
        gy = yf * gate
        dyn = R.dyn[rows, tok].astype(f32)
        gyr = gy * r
        R.accx[5, rows, :] += fold(dyn * gyr)
        dgy = (r * wide(R.px, 5, rows)) * dyn - gy * rs
        R.dcat[rows, tok] = (dgy * yf * (sz + gate * (1.0 - sz))).astype(bf16)
        dy = dgy * gate
        dyb = dy.astype(bf16)
        R.accx[6, rows, :] += fold(dy * x)
        xd = x * dt[hh, :]
        xdb = xd.astype(bf16)
        d = jnp.exp(jnp.minimum(l_col[:, hh] - l_row[hh, :], 0.0))
        mix = (d * R.gm[...]).astype(bf16)
        vin = nn(dyb, mix)
        dm = tn(dyb, xdb) * d
        if h == 0:
            R.dg[...] = dm
        else:
            R.dg[...] += dm
        stb = R.states[b, rows, :]
        lam = R.state[rows, :]
        lamb = lam.astype(bf16)
        lb = nn(lamb, bt) * we[hh, :]
        vt = vin + lb
        xlow = xdb.astype(f32)
        decays.append(jnp.sum(dyb.astype(f32) * y - xlow * vt, axis=0, keepdims=True))
        directs.append(jnp.sum(x * vt, axis=0, keepdims=True))
        through = jnp.sum(lam * stb.astype(f32), axis=0, keepdims=True) * kept[hh, :]
        ends.append(
            jnp.sum(xlow * lb, axis=0, keepdims=True)
            + jnp.concatenate([through, jnp.zeros((1, SPAN - STATE), f32)], axis=1)
        )
        edy = (dy * e[hh, :]).astype(bf16)
        R.edy[rows, :] = edy
        R.wxd[rows, :] = (xd * we[hh, :]).astype(bf16)
        R.lamb[rows, :] = lamb
        R.state[rows, :] = kept[hh, :] * lam + nt(edy, ct)
        dx = dt[hh, :] * vt + skip * dy
        du = dx * (sx + x * (1.0 - sx))
        conv_backward(R, R.xr[rows, tok].astype(f32), du, R.px, R.accx, R.head_x, rows, C, tok, m)
    dgm = (R.dg[...] * mask).astype(bf16)
    dct = nt(bt, dgm) + tn(R.states[b], R.edy[...])
    dbt = nn(ct, dgm) + tn(R.lamb[...], R.wxd[...])
    du = jnp.concatenate([dbt, dct], axis=0) * (sg + ubc * sg * (1.0 - sg))
    conv_backward(
        R, R.bcr[:, tok].astype(f32), du, R.pbc, R.accbc, R.head_bc, slice(0, BC), 2 * C, tok, m
    )
    pad = [jnp.zeros((8 - H, SPAN), f32)]
    end = jnp.sum(jnp.concatenate(ends + pad, axis=0), axis=1, keepdims=True)
    g = merge3(nn(split3(jnp.concatenate(decays + pad, axis=0)), tri_low())) + end
    ddr = (g * rate + jnp.concatenate(directs + pad, axis=0)) * jax.nn.sigmoid(v)
    R.acch[0] += ddr
    R.acch[1] += g * dt * rate
    R.dcat[2 * C + BC : 2 * C + BC + 16, tok] = jnp.concatenate(
        [ddr, jnp.zeros((8, SPAN), f32)], axis=0
    ).astype(bf16)


def remote(src, dst, send, recv, device):
    return pltpu.make_async_remote_copy(
        src_ref=src, dst_ref=dst, send_sem=send, recv_sem=recv, device_id=device, device_id_type=MESH
    )


class Place:
    def __init__(self, n):
        self.n = n
        self.dp, self.row, self.col = (lax.axis_index(a) for a in ("dp", "row", "col"))
        self.x, self.c, self.y = self.row // 2, self.row % 2, self.col
        self.q = self.index(self.x, self.c, self.y)
        self.mate = (self.dp, self.x * 2 + 1 - self.c, self.y)
        self.xn = (self.dp, (1 - self.x) * 2 + self.c, self.y)
        self.yn = (self.dp, self.row, 1 - self.y)
        self.diag = (self.dp, (1 - self.x) * 2 + self.c, 1 - self.y)

    def index(self, x, c, y):
        return (x * 2 + c) * 2 + y

    def plane(self, d):
        k = (self.q + d) % 8
        return k, (self.dp, k // 2, k % 2)

    def line(self, d):
        k = (self.dp + d) % self.n
        return k, (k, self.row, self.col)

    def right(self):
        return (self.dp + 1, self.row, self.col)

    def left(self):
        return (self.dp - 1, self.row, self.col)


class PlaneGather:
    def __init__(self, me, buf, send, recv):
        self.me, self.buf, self.send, self.recv = me, buf, send, recv
        x, c, y = me.x, me.c, me.y
        own = lambda cc: (
            me.index(x, cc, y),
            me.index(1 - x, cc, y),
            me.index(x, cc, 1 - y),
            me.index(1 - x, cc, 1 - y),
        )
        self.q, self.qx, self.qy, self.qd = own(c)
        self.mq, self.mx, self.my, self.md = own(1 - c)

    def at(self, k, half):
        if half is None:
            return self.buf.at[aligned(k * SPAN, SPAN), :]
        return self.buf.at[aligned(k * SPAN + half * HALF, HALF), :]

    def copy(self, i, k, half, device):
        region = self.at(k, half)
        return remote(region, region, self.send.at[i], self.recv.at[i], device)

    def wait(self, i, k, half):
        self.copy(i, k, half, self.me.mate).wait_recv()

    def start(self):
        me = self.me
        self.copy(0, self.q, 0, me.xn).start()
        self.copy(3, self.q, 1, me.yn).start()
        self.copy(1, self.q, 1, me.xn).start()
        self.copy(2, self.q, 0, me.yn).start()
        self.copy(6, self.q, None, me.mate).start()

    def step1(self):
        me = self.me
        self.wait(0, self.qx, 0)
        self.copy(4, self.qx, 0, me.yn).start()
        self.copy(7, self.qx, 0, me.mate).start()
        self.wait(3, self.qy, 1)
        self.copy(5, self.qy, 1, me.xn).start()
        self.copy(10, self.qy, 1, me.mate).start()

    def step2(self):
        me = self.me
        self.wait(1, self.qx, 1)
        self.copy(8, self.qx, 1, me.mate).start()
        self.wait(2, self.qy, 0)
        self.copy(9, self.qy, 0, me.mate).start()

    def step3(self):
        me = self.me
        self.wait(4, self.qd, 0)
        self.copy(11, self.qd, 0, me.mate).start()
        self.wait(5, self.qd, 1)
        self.copy(12, self.qd, 1, me.mate).start()

    def step4(self):
        self.wait(6, self.mq, None)
        self.wait(7, self.mx, 0)
        self.wait(8, self.mx, 1)
        self.wait(9, self.my, 0)
        self.wait(10, self.my, 1)
        self.wait(11, self.md, 0)
        self.wait(12, self.md, 1)
        for i in range(13):
            self.copy(i, self.q, None if i == 6 else 0, self.me.mate).wait_send()


def both(*conds):
    out = conds[0]
    for c in conds[1:]:
        out = jnp.logical_and(out, c)
    return out


class LineGather:
    def __init__(self, me, at, send, recv):
        self.me, self.at, self.send, self.recv = me, at, send, recv

    def copy(self, way, s, k):
        device = self.me.right() if way == 0 else self.me.left()
        return remote(self.at(k), self.at(k), self.send.at[way, s], self.recv.at[way, s], device)

    def start(self):
        me = self.me

        @pl.when(me.dp < me.n - 1)
        def _():
            self.copy(0, 0, me.dp).start()

        @pl.when(me.dp > 0)
        def _():
            self.copy(1, 0, me.dp).start()

    def step(self, s):
        me = self.me
        k = me.dp - 1 - s

        @pl.when(k >= 0)
        def _():
            self.copy(0, s, k).wait_recv()

            @pl.when(both(me.dp < me.n - 1, s < me.n - 2))
            def _():
                self.copy(0, s + 1, k).start()

        j = me.dp + 1 + s

        @pl.when(j <= me.n - 1)
        def _():
            self.copy(1, s, j).wait_recv()

            @pl.when(both(me.dp > 0, s < me.n - 2))
            def _():
                self.copy(1, s + 1, j).start()

    def finish(self, s):
        me = self.me

        @pl.when(both(me.dp < me.n - 1, me.dp - s >= 0))
        def _():
            self.copy(0, s, me.dp).wait_send()

        @pl.when(both(me.dp > 0, me.dp + s <= me.n - 1))
        def _():
            self.copy(1, s, me.dp).wait_send()


class LineScatter:
    def __init__(self, me, src, slot, send, recv):
        self.me, self.src, self.slot, self.send, self.recv = me, src, slot, send, recv

    def copy(self, way, s, what, to):
        (a, i), (b, j) = what, to
        device = self.me.right() if way == 0 else self.me.left()
        return remote(a.at[i], b.at[j], self.send.at[way, s], self.recv.at[way, s], device)

    def got(self, way, s, slot):
        self.copy(way, s, slot, slot).wait_recv()

    def add(self, k):
        (a, i), (b, j) = self.slot(k), self.src(k)
        a[i] = (a[i].astype(f32) + b[j].astype(f32)).astype(bf16)

    def step(self, s):
        me, n = self.me, self.me.n
        k = n - 1 - s

        @pl.when(k > me.dp)
        def _():
            @pl.when(me.dp > 0)
            def _():
                self.got(0, s, self.slot(k))
                self.add(k)
                self.copy(0, s, self.slot(k), self.slot(k)).start()

            @pl.when(me.dp == 0)
            def _():
                self.copy(0, s, self.src(k), self.slot(k)).start()

        j = s

        @pl.when(j < me.dp)
        def _():
            to = self.slot(jnp.where(j == me.dp - 1, n, j))

            @pl.when(me.dp < n - 1)
            def _():
                self.got(1, s, self.slot(j))
                self.add(j)
                self.copy(1, s, self.slot(j), to).start()

            @pl.when(me.dp == n - 1)
            def _():
                self.copy(1, s, self.src(j), to).start()

    def total(self, put):
        me, n = self.me, self.me.n
        a, i = self.src(me.dp)
        put(a[i].astype(f32), True)

        @pl.when(me.dp > 0)
        def _():
            b, j = self.slot(me.dp)
            self.got(0, n - 1 - me.dp, (b, j))
            put(b[j].astype(f32), False)

        @pl.when(me.dp < n - 1)
        def _():
            b, j = self.slot(n)
            self.got(1, me.dp, (b, j))
            put(b[j].astype(f32), False)

    def finish(self, s):
        me, n = self.me, self.me.n

        @pl.when(s < n - 1 - me.dp)
        def _():
            self.copy(0, s, self.src(0), self.slot(0)).wait_send()

        @pl.when(s < me.dp)
        def _():
            self.copy(1, s, self.src(0), self.slot(0)).wait_send()


class PlaneScatter:
    def __init__(self, me, R, send, recv, part, credit):
        self.me, self.R, self.send, self.recv, self.part, self.credit = me, R, send, recv, part, credit
        x, y = me.x, me.y
        self.jo, self.jx, self.jy, self.jd = x * 2 + y, (1 - x) * 2 + y, x * 2 + 1 - y, (1 - x) * 2 + 1 - y

    def copy(self, i, src, dst, device):
        return remote(src, dst, self.send.at[i], self.recv.at[i], device)

    def first(self):
        me, R = self.me, self.R
        if self.credit:
            pl.semaphore_wait(R.free.at[0], 1)

        @pl.loop(0, 4)
        def _(j):
            k = me.index(j // 2, 1 - me.c, j % 2)

            @pl.when(j >= 2)
            def _():
                self.copy(j - 2, R.sb.at[j % 2], R.rb.at[j - 2], me.mate).wait_send()

            R.sb[j % 2, 0] = self.part(k, 0).astype(bf16)
            R.sb[j % 2, 1] = self.part(k, 1).astype(bf16)
            self.copy(j, R.sb.at[j % 2], R.rb.at[j], me.mate).start()

    def second(self):
        me, R = self.me, self.R
        if self.credit:
            pl.semaphore_wait(R.free.at[1], 1)
            pl.semaphore_wait(R.free.at[2], 1)

        @pl.loop(0, 4)
        def _(t):
            dx, dy = 1 - t // 2, 1 - t % 2
            xx = me.x + dx * (1 - 2 * me.x)
            yy = me.y + dy * (1 - 2 * me.y)
            j = xx * 2 + yy
            k = me.index(xx, me.c, yy)
            self.copy(j, R.sb.at[0], R.rb.at[j], me.mate).wait_recv()
            R.rb[j, 0] = (self.part(k, 0) + R.rb[j, 0].astype(f32)).astype(bf16)
            R.rb[j, 1] = (self.part(k, 1) + R.rb[j, 1].astype(f32)).astype(bf16)

            @pl.when(t == 0)
            def _():
                self.copy(4, R.rb.at[self.jd, 0], R.da, me.xn).start()
                self.copy(5, R.rb.at[self.jd, 1], R.db, me.yn).start()

            @pl.when(t == 1)
            def _():
                self.copy(6, R.rb.at[self.jx, 0], R.fx.at[0], me.xn).start()

            @pl.when(t == 2)
            def _():
                self.copy(9, R.rb.at[self.jy, 1], R.fy.at[1], me.yn).start()

    def relay(self):
        me, R = self.me, self.R
        self.copy(4, R.da, R.da, me.xn).wait_recv()
        R.rb[self.jy, 0] = (R.rb[self.jy, 0].astype(f32) + R.da[...].astype(f32)).astype(bf16)
        self.copy(8, R.rb.at[self.jy, 0], R.fy.at[0], me.yn).start()
        self.copy(5, R.db, R.db, me.yn).wait_recv()
        R.rb[self.jx, 1] = (R.rb[self.jx, 1].astype(f32) + R.db[...].astype(f32)).astype(bf16)
        self.copy(7, R.rb.at[self.jx, 1], R.fx.at[1], me.xn).start()

    def total(self, put):
        me, R = self.me, self.R
        for half in (0, 1):
            self.copy(6 + half, R.fx.at[half], R.fx.at[half], me.xn).wait_recv()
            self.copy(8 + half, R.fy.at[half], R.fy.at[half], me.yn).wait_recv()
            steps = R.da.shape[0] // 128

            @pl.loop(0, steps)
            def _(i):
                rows = aligned(i * 128, 128)
                v = R.rb[self.jo, half, rows, :].astype(f32)
                put(half * steps + i, v + R.fx[half, rows, :].astype(f32) + R.fy[half, rows, :].astype(f32))

    def finish(self, release):
        me, R = self.me, self.R
        for i in (2, 3):
            self.copy(i, R.sb.at[i % 2], R.rb.at[i], me.mate).wait_send()
        for i in range(4, 10):
            self.copy(i, R.da, R.db, me.mate).wait_send()
        if release:
            for i, device in enumerate((me.mate, me.xn, me.yn)):
                pl.semaphore_signal(R.free.at[i], 1, device_id=device, device_id_type=MESH)


def stepped(n, *fns):
    if n <= 4:
        return [lambda s=s: [f(s) for f in fns] for s in range(n - 1)]

    def every():
        @pl.loop(0, n - 1)
        def _(s):
            for f in fns:
                f(s)

    return [every] + [lambda: None] * 2


def kernel(names, n, C, H, inner, *refs):
    R = types.SimpleNamespace(**dict(zip(names, refs)))
    me = Place(n)
    T, D = R.hn.shape
    nb = T // SPAN
    DS = D // n
    dp = me.dp
    dt_rows = slice(2 * C + BC, 2 * C + BC + 16)
    mine = aligned(me.q * SPAN, SPAN)
    share = lambda k: pl.ds(pl.multiple_of(k * DS, 16), DS)
    dhalf = lambda h: slice(h * (D // 2), (h + 1) * (D // 2))
    half = aligned(2 * C + me.c * 128, 128)
    other = aligned(2 * C + (1 - me.c) * 128, 128)

    barrier = pltpu.get_barrier_semaphore()
    for d in range(1, 8):
        pl.semaphore_signal(barrier, 1, device_id=me.plane(d)[1], device_id_type=MESH)
    for d in range(1, n):
        pl.semaphore_signal(barrier, 1, device_id=me.line(d)[1], device_id_type=MESH)

    stage = lambda a, z: R.y.at[0:DS, a:z]
    arriving = [
        pltpu.make_async_copy(src, dst, R.loc.at[i])
        for i, (src, dst) in enumerate(
            (
                (R.wx, stage(C, 2 * C)),
                (R.wbc, stage(2 * C, 2 * C + BC)),
                (R.wz, stage(0, C)),
                (R.gcot, R.cot.at[mine, :]),
            )
        )
    ]
    for copy in arriving:
        copy.start()
    @pl.loop(0, SPAN // 32)
    def _(i):
        u = R.hid[aligned(i * 32, 32), :].astype(f32)
        qn = lax.rsqrt(jnp.mean(u * u, axis=1, keepdims=True) + EPS)
        R.hn[aligned(me.q * SPAN + i * 32, 32), :] = (u * qn * R.gain[...]).astype(bf16)

    for copy in arriving:
        copy.wait()
    R.wd[share(dp), 0 : 2 * C] = R.y[0:DS, 0 : 2 * C].astype(bf16)
    R.wd[share(dp), half] = R.y[0:DS, half].astype(bf16)
    R.wot[share(dp), :] = R.wo[...].T.astype(bf16)
    R.wdt[dp] = R.wdt_own[...]
    pl.semaphore_wait(barrier, 7 + n - 1)

    tokens = PlaneGather(me, R.hn, R.ag_s.at[0], R.ag_r.at[0])
    cots = PlaneGather(me, R.cot, R.ag_s.at[1], R.ag_r.at[1])
    places = (
        lambda k: R.wd.at[share(k), C : 2 * C],
        lambda k: R.wd.at[share(k), half],
        lambda k: R.wdt.at[k],
        lambda k: R.wd.at[share(k), 0:C],
        lambda k: R.wot.at[share(k), :],
    )
    gathers = [LineGather(me, at, R.za_s.at[i], R.za_r.at[i]) for i, at in enumerate(places)]
    first, wo_gather = gathers[:4], gathers[4]
    tokens.start()
    for g in first:
        g.start()

    for k in range(7):
        R.px[k] = jnp.broadcast_to(R.pxc[:, k : k + 1], (C, 128))
    for k in range(5):
        R.pbc[k] = jnp.broadcast_to(R.pbcc[:, k : k + 1], (BC, 128))
    for a in (R.tail_bc, R.tail_x, R.state, R.head_x, R.head_bc, R.accx, R.accbc, R.acch, R.sv):
        a[...] = jnp.zeros_like(a)
    offs = [R.offs[k] for k in range(R.offs.shape[0])]

    line = stepped(n, *[g.step for g in first])
    tokens.step1()
    line[0]()
    tokens.step2()
    line[1]()
    tokens.step3()
    cots.start()
    line[2]()
    bc_swap = remote(R.wd.at[:, half], R.wd.at[:, half], R.mate_s.at[0], R.mate_r.at[0], me.mate)
    bc_swap.start()
    wo_gather.start()
    tokens.step4()
    remote(R.wd.at[:, other], R.wd.at[:, other], R.mate_s.at[0], R.mate_r.at[0], me.mate).wait_recv()
    bc_swap.wait_send()
    for s in stepped(n, *[g.finish for g in first]):
        s()
    for k in range(0, 2 * C + BC, 256):
        R.wcat[k : k + 256, :] = R.wd[:, k : k + 256].T
    for k in range(n):
        R.wcat[dt_rows, k * DS : (k + 1) * DS] = R.wdt[k]
    pad = jnp.zeros((112, D), bf16)
    R.wd[:, 2 * C + BC : 2 * C + BC + 128] = jnp.concatenate([R.wcat[dt_rows, :], pad], axis=0).T

    line = stepped(n, wo_gather.step)
    beside = {3: [cots.step1, line[0]], 5: [line[1]], 6: [cots.step2], 7: [line[2]]}

    @pl.loop(0, nb)
    def _(b):
        fwd_block(b, R, offs, C, H)
        for k, fns in beside.items():

            @pl.when(b == min(k, nb - 1))
            def _():
                for f in fns:
                    f()

    cots.step3()
    cots.step4()
    for s in stepped(n, wo_gather.finish):
        s()
    for k in range(0, D, 256):
        R.wout[:, k : k + 256] = R.wot[k : k + 256, :].T

    @pl.loop(0, nb)
    def _(b):
        tok = aligned(b * SPAN, SPAN)
        dyn = nt(R.wout[...], R.cot[tok, :])
        R.dyn[:, tok] = dyn.astype(bf16)
        R.sums[pl.ds(nb + b, 1), :] = jnp.sum(dyn * R.gg[:, tok].astype(f32), axis=0, keepdims=True)

    for d in range(1, 8):
        k, device = me.plane(d)
        remote(R.sums, R.sslot.at[me.q], R.sum_s.at[k], R.sum_r.at[me.q], device).start()
    R.sslot[me.q] = R.sums[...]

    mixed = PlaneScatter(
        me, R, R.rs_s.at[0], R.rs_r.at[0], lambda k, h: nn(R.wot[dhalf(h), :], R.gg[:, aligned(k * SPAN, SPAN)]), False
    )
    mixed.first()
    mixed.second()
    for d in range(1, 8):
        k, device = me.plane(d)
        remote(R.sums, R.sslot.at[k], R.sum_s.at[k], R.sum_r.at[k], device).wait()
    total = R.sslot[0]
    for k in range(1, 8):
        total = total + R.sslot[k]
    R.tot[...] = total

    @pl.loop(0, nb)
    def _(b):
        tok = aligned(b * SPAN, SPAN)
        r = lax.rsqrt(R.tot[pl.ds(b, 1), :] / inner + EPS)
        R.gg[:, tok] = (R.gg[:, tok].astype(f32) * r).astype(bf16)

    @pl.loop(0, D // 256)
    def _(i):
        some = aligned(i * 256, 256)
        R.wot[some, :] = nn(R.gg[...], R.cot[:, some]).astype(bf16).T

    @pl.when(dp < n - 1)
    def _():
        pl.semaphore_signal(R.free.at[3], 1, device_id=me.right(), device_id_type=MESH)

    @pl.when(dp > 0)
    def _():
        pl.semaphore_signal(R.free.at[4], 1, device_id=me.left(), device_id_type=MESH)

    @pl.when(dp > 0)
    def _():
        pl.semaphore_wait(R.free.at[3], 1)

    @pl.when(dp < n - 1)
    def _():
        pl.semaphore_wait(R.free.at[4], 1)

    def scatter(i, src, lanes):
        slot = lambda k: (R.cot, (share(k), slice(*lanes)))
        return LineScatter(me, src, slot, R.zr_s.at[i], R.zr_r.at[i])

    wo_sum = scatter(0, lambda k: (R.wot, (share(k), slice(0, C))), (2 * C + 128, 3 * C + 128))
    x_sum = scatter(1, lambda k: (R.wd, (share(k), slice(C, 2 * C))), (C, 2 * C))
    z_sum = scatter(2, lambda k: (R.wd, (share(k), slice(0, C))), (0, C))
    bc_sum = scatter(3, lambda k: (R.wd, (share(k), half)), (2 * C, 2 * C + 128))
    dt_sum = LineScatter(
        me, lambda k: (R.gdt, (k,)), lambda k: (R.rdt, (k,)), R.zr_s.at[4], R.zr_r.at[4]
    )

    def put(ref):
        def f(v, new):
            if new:
                ref[...] = v
            else:
                ref[...] += v

        return f

    out_copy = pltpu.make_async_copy(R.wout.at[0:SPAN, :], R.block_out, R.loc.at[5])

    def finish_mixed():
        r = lax.rsqrt(R.tot[pl.ds(me.q, 1), :] / inner + EPS)

        def put(k, v):
            cols = aligned(k * 128, 128)
            R.wout[0:SPAN, cols] = (R.hid[:, cols].astype(f32) + (v * r).T).astype(bf16)

        mixed.total(put)
        out_copy.start()
        mixed.finish(True)

    R.state[...] = jnp.zeros_like(R.state)
    line = stepped(n, wo_sum.step)
    beside = {1: [mixed.relay, line[0]], 3: [line[1]], 5: [line[2]], 6: [finish_mixed]}

    @pl.loop(0, nb)
    def _(i):
        bwd_block(nb - 1 - i, R, offs, C, H, inner)
        for k, fns in beside.items():

            @pl.when(i == min(k, nb - 1))
            def _():
                for f in fns:
                    f()

    rows = 2 * C + BC + 16
    dhn = PlaneScatter(
        me,
        R,
        R.rs_s.at[1],
        R.rs_r.at[1],
        lambda k, h: nn(R.wd[dhalf(h), 0:rows], R.dcat[:, aligned(k * SPAN, SPAN)]),
        True,
    )
    dhn.first()
    dhn.second()

    def weight_grad(a, z):
        @pl.loop(0, D // 256)
        def _(i):
            some = aligned(i * 256, 256)
            g = nn(R.dcat[a:z, :], R.hn[:, some])
            R.ng[:, some] += jnp.sum(g * R.wcat[a:z, some].astype(f32), axis=0, keepdims=True)
            g = g.astype(bf16)
            R.wd[some, a : a + 256] = g[0:256].T
            if z - a > 256:
                R.gdt_all[:, some] = g[256:272]

    R.ng[...] = jnp.zeros_like(R.ng)
    weight_grad(2 * C, rows)
    for k in range(n):
        R.gdt[k] = R.gdt_all[:, k * DS : (k + 1) * DS]
    bx = R.cot.at[0:D, 3 * C + 128 : 3 * C + 256]
    bc_pair = remote(R.wd.at[:, other], bx, R.mate_s.at[1], R.mate_r.at[1], me.mate)
    bc_pair.start()
    for a in (2 * C - 256, 2 * C - 512):
        weight_grad(a, a + 256)
    bc_pair.wait()
    R.wd[:, half] = (R.wd[:, half].astype(f32) + bx[...].astype(f32)).astype(bf16)
    line = stepped(n, x_sum.step, bc_sum.step, dt_sum.step)
    line[0]()
    dhn.relay()
    for a in range(2 * C - 768, -1, -256):
        weight_grad(a, a + 256)
    zline = stepped(n, z_sum.step)
    zline[0]()

    ax = [jnp.sum(R.accx[k], axis=1, keepdims=True) for k in range(7)]
    ab = [jnp.sum(R.accbc[k], axis=1, keepdims=True) for k in range(5)]
    R.sv[0:8, :] = jnp.concatenate(ax + [jnp.zeros((C, 1), f32)], axis=1).T
    R.sv[8:16, 0:BC] = jnp.concatenate(ab + [jnp.zeros((BC, 3), f32)], axis=1).T
    ng = R.ng[...] / R.gain[...]
    for k in range(D // C):
        R.sv[16 + k : 17 + k, :] = ng[:, k * C : (k + 1) * C]
    for k in range(2):
        R.sv[24 + 8 * k : 32 + 8 * k, 0:128] = jnp.broadcast_to(
            jnp.sum(R.acch[k], axis=1, keepdims=True), (8, 128)
        )
    for d in range(1, n):
        k, device = me.line(d)
        remote(R.sv, R.lslot.at[dp], R.ls_s.at[k], R.ls_r.at[dp], device).start()
    R.lslot[dp] = R.sv[...]
    line[1]()
    zline[1]()
    for d in range(1, n):
        k, device = me.line(d)
        remote(R.sv, R.lslot.at[k], R.ls_s.at[k], R.ls_r.at[k], device).wait()
    total = R.lslot[0]
    for k in range(1, n):
        total = total + R.lslot[k]
    R.pv[...] = total
    for d in range(1, 8):
        k, device = me.plane(d)
        remote(R.pv, R.small.at[me.q], R.ps_s.at[k], R.ps_r.at[me.q], device).start()
    R.small[me.q] = total
    line[2]()
    zline[2]()

    x_sum.total(put(R.gx))
    bc_sum.total(put(R.bsum))
    j = me.x * 2 + me.y
    R.bslot[j] = R.bsum[...].astype(bf16)
    crossing = []
    for i, (device, k) in enumerate(
        ((me.xn, (1 - me.x) * 2 + me.y), (me.yn, me.x * 2 + 1 - me.y), (me.diag, (1 - me.x) * 2 + 1 - me.y))
    ):
        remote(R.bslot.at[j], R.bslot.at[j], R.bc_s.at[i], R.bc_r.at[i], device).start()
        crossing.append(remote(R.bslot.at[k], R.bslot.at[k], R.bc_s.at[i], R.bc_r.at[i], device))
    z_sum.total(put(R.gz))
    dt_sum.total(put(R.gdt_out))
    wo_sum.total(put(R.gwo))
    for c in crossing:
        c.wait()
    v = R.bslot[0].astype(f32)
    for k in range(1, 4):
        v = v + R.bslot[k].astype(f32)
    R.bfin[me.c] = v.astype(bf16)
    bc_last = remote(R.bfin.at[me.c], R.bfin.at[me.c], R.mate_s.at[2], R.mate_r.at[2], me.mate)
    bc_last.start()

    cot_again = pltpu.make_async_copy(R.gcot, R.hn.at[0:SPAN, :], R.loc.at[4])
    cot_again.start()
    def put_dh(k, v):
        R.y[0:SPAN, aligned(k * 128, 128)] = v.T

    dhn.total(put_dh)
    cot_again.wait()

    @pl.loop(0, SPAN // 32)
    def _(i):
        some = aligned(i * 32, 32)
        u = R.hid[some, :].astype(f32)
        qn = lax.rsqrt(jnp.mean(u * u, axis=1, keepdims=True) + EPS)
        w = R.y[some, 0:D] * R.gain[...]
        dot = jnp.sum(w * u, axis=1, keepdims=True) / D
        R.hn[aligned(SPAN + i * 32, 32), :] = (R.hn[some, :].astype(f32) + qn * w - u * (qn * qn * qn * dot)).astype(bf16)

    in_copy = pltpu.make_async_copy(R.hn.at[SPAN : 2 * SPAN, :], R.grad_in, R.loc.at[6])
    in_copy.start()
    bc_last.wait_send()
    remote(
        R.bfin.at[1 - me.c], R.bfin.at[1 - me.c], R.mate_s.at[2], R.mate_r.at[2], me.mate
    ).wait_recv()
    R.gbc[:, 0:128] = R.bfin[0].astype(f32)
    R.gbc[:, 128:256] = R.bfin[1].astype(f32)
    for d in range(1, 8):
        k, device = me.plane(d)
        remote(R.pv, R.small.at[k], R.ps_s.at[k], R.ps_r.at[k], device).wait()
    dhn.finish(False)
    in_copy.wait()
    out_copy.wait()
    for fin in (wo_sum, x_sum, z_sum, bc_sum, dt_sum):
        for s in stepped(n, fin.finish):
            s()


def shards(
    n,
    hidden_in,
    lengths,
    perm,
    norm_gain,
    w_z,
    w_x,
    w_dt,
    w_bc,
    conv_x,
    conv_x_bias,
    conv_bc,
    conv_bc_bias,
    dt_bias,
    a_log,
    skip_d,
    gate_gain,
    w_out,
    grad_out,
):
    place = lax.axis_index("row") * lax.axis_size("col") + lax.axis_index("col")
    rows, D = hidden_in.shape
    T = rows * 8
    DS, C = w_z.shape
    H = w_dt.shape[1]
    inner = gate_gain.shape[0]
    nb = T // SPAN
    wide_rows = 2 * C + BC + 16

    dealt = jnp.sum(
        jnp.where(perm[:, None] == jnp.arange(lengths.shape[0])[None, :], lengths[None, :], 0), axis=1
    )
    offs = (jnp.cumsum(dealt) - dealt).astype(jnp.int32)
    px = jnp.concatenate(
        [
            conv_x,
            conv_x_bias[None],
            gate_gain[None],
            jnp.repeat(skip_d, inner // skip_d.shape[0])[None],
            jnp.zeros((1, inner), f32),
        ],
        axis=0,
    )
    px = lax.dynamic_slice_in_dim(px, place * C, C, 1).T
    pbc = jnp.concatenate([conv_bc, conv_bc_bias[None], jnp.zeros((3, BC), f32)], axis=0).T
    ph = jnp.stack([dt_bias, -jnp.exp(a_log)], axis=1)
    ph = jnp.pad(lax.dynamic_slice_in_dim(ph, place * H, H, 0), ((0, 8 - H), (0, 6)))
    wdt = jnp.pad(w_dt.astype(bf16).T, ((0, 16 - H), (0, 0)))

    inputs = dict(
        hid=hidden_in,
        gcot=grad_out,
        wz=w_z,
        wx=w_x,
        wbc=w_bc,
        wdt_own=wdt,
        wo=w_out,
        gain=norm_gain[None],
        pxc=px,
        pbcc=pbc,
        ph=ph,
        offs=offs,
    )
    outputs = dict(
        block_out=((rows, D), bf16),
        grad_in=((rows, D), bf16),
        gz=((DS, C), f32),
        gx=((DS, C), f32),
        gbc=((DS, BC), f32),
        gdt_out=((16, DS), f32),
        gwo=((DS, C), f32),
        small=((8, 40, C), f32),
    )
    scratch = dict(
        hn=((T, D), bf16),
        cot=((T, D), bf16),
        wd=((D, 2 * C + BC + 128), bf16),
        wcat=((wide_rows, D), bf16),
        wot=((D, C), bf16),
        wout=((C, D), bf16),
        wdt=((n, 16, DS), bf16),
        pr=((wide_rows, SPAN), f32),
        z=((C, T), bf16),
        xr=((C, T), bf16),
        bcr=((BC, T), bf16),
        ux=((C, T), bf16),
        ubc=((BC, T), bf16),
        dr=((8, T), f32),
        y=((C, T), f32),
        gg=((C, T), bf16),
        dyn=((C, T), bf16),
        dcat=((wide_rows, T), bf16),
        states=((nb, C, STATE), bf16),
        state=((C, STATE), f32),
        gm=((SPAN, SPAN), f32),
        dg=((SPAN, SPAN), f32),
        edy=((C, SPAN), bf16),
        wxd=((C, SPAN), bf16),
        lamb=((C, STATE), bf16),
        tail_x=((C, 128), f32),
        tail_bc=((BC, 128), f32),
        head_x=((3, C, 128), f32),
        head_bc=((3, BC, 128), f32),
        px=((7, C, 128), f32),
        pbc=((5, BC, 128), f32),
        accx=((7, C, 128), f32),
        accbc=((5, BC, 128), f32),
        acch=((2, 8, SPAN), f32),
        sums=((2 * nb, SPAN), f32),
        tot=((2 * nb, SPAN), f32),
        sslot=((8, 2 * nb, SPAN), f32),
        sb=((2, 2, D // 2, SPAN), bf16),
        rb=((4, 2, D // 2, SPAN), bf16),
        da=((D // 2, SPAN), bf16),
        db=((D // 2, SPAN), bf16),
        fx=((2, D // 2, SPAN), bf16),
        fy=((2, D // 2, SPAN), bf16),
        gdt_all=((16, D), bf16),
        gdt=((n, 16, DS), bf16),
        rdt=((n + 1, 16, DS), bf16),
        bsum=((DS, 128), f32),
        bslot=((4, DS, 128), bf16),
        bfin=((2, DS, 128), bf16),
        ng=((1, D), f32),
        sv=((40, C), f32),
        pv=((40, C), f32),
        lslot=((n, 40, C), f32),
    )
    semaphores = dict(
        ag_s=(2, 13),
        ag_r=(2, 13),
        za_s=(5, 2, n - 1),
        za_r=(5, 2, n - 1),
        zr_s=(5, 2, n - 1),
        zr_r=(5, 2, n - 1),
        rs_s=(2, 10),
        rs_r=(2, 10),
        mate_s=(3,),
        mate_r=(3,),
        sum_s=(8,),
        sum_r=(8,),
        ls_s=(n,),
        ls_r=(n,),
        ps_s=(8,),
        ps_r=(8,),
        bc_s=(3,),
        bc_r=(3,),
        loc=(7,),
    )
    names = [*inputs, *outputs, *scratch, *semaphores, "free"]
    vmem = pl.BlockSpec(memory_space=pltpu.VMEM)
    where = {k: pl.BlockSpec(memory_space=pl.ANY) for k in ("gcot", "wz", "wx", "wbc", "block_out", "grad_in")}
    where["offs"] = pl.BlockSpec(memory_space=pltpu.SMEM)
    out = pl.pallas_call(
        functools.partial(kernel, names, n, C, H, float(inner)),
        out_shape=[jax.ShapeDtypeStruct(*s) for s in outputs.values()],
        in_specs=[where.get(k, vmem) for k in inputs],
        out_specs=[where.get(k, vmem) for k in outputs],
        scratch_shapes=[pltpu.VMEM(*s) for s in scratch.values()]
        + [pltpu.SemaphoreType.DMA(s) for s in semaphores.values()]
        + [pltpu.SemaphoreType.REGULAR((5,))],
        compiler_params=pltpu.CompilerParams(
            collective_id=0, has_side_effects=True, vmem_limit_bytes=(64 << 20) - (1 << 18)
        ),
    )(*inputs.values())
    o = types.SimpleNamespace(**dict(zip(outputs, out)))
    own = o.small[:, 0:8, :].transpose(1, 0, 2).reshape(8, inner)
    shared = jnp.sum(o.small[:, 8:24, :], axis=0)
    heads = o.small[:, 24:40, 0].reshape(8, 2, 8)[:, :, 0:H].transpose(1, 0, 2).reshape(2, -1)
    return (
        o.block_out,
        o.grad_in,
        shared[8 : 8 + D // C].reshape(D),
        o.gz,
        o.gx,
        o.gdt_out[0:H].T,
        o.gbc,
        own[0:4],
        own[4],
        shared[0:4, 0:BC],
        shared[4, 0:BC],
        heads[0],
        heads[1],
        jnp.sum(own[6].reshape(skip_d.shape[0], -1), axis=1),
        own[5],
        o.gwo.T,
    )


def solution(mesh):
    assert mesh.shape["row"] == 4 and mesh.shape["col"] == 2
    every = P(("dp", "row", "col"), None)
    weight = P("dp", ("row", "col"))
    out = P(("row", "col"), "dp")
    return jax.shard_map(
        functools.partial(shards, mesh.shape["dp"]),
        mesh=mesh,
        in_specs=(every, P(), P("dp"), P(), weight, weight, weight, P("dp", None))
        + (P(),) * 8
        + (out, every),
        out_specs=(every, every, P(), weight, weight, weight, P("dp", None)) + (P(),) * 8 + (out,),
        check_vma=False,
    )
```

```python
import functools
import types

import jax
import jax.numpy as jnp
from jax import lax
from jax.experimental import pallas as pl
from jax.experimental.pallas import tpu as pltpu
from jax.sharding import PartitionSpec as P

SPAN = 256
HALF = SPAN // 2
STATE = 128
BC = 2 * STATE
KERNEL = 4
EPS = 1e-5
f32, bf16 = jnp.float32, jnp.bfloat16
MESH = pl.DeviceIdType.MESH


def nt(a, b):
    return lax.dot_general(a, b, (((1,), (1,)), ((), ())), preferred_element_type=f32)


def nn(a, b):
    return lax.dot_general(a, b, (((1,), (0,)), ((), ())), preferred_element_type=f32)


def tn(a, b):
    return lax.dot_general(a, b, (((0,), (0,)), ((), ())), preferred_element_type=f32)


def aligned(start, size):
    return pl.ds(pl.multiple_of(start, size), size)


def softplus(v):
    return jnp.maximum(v, 0.0) + jnp.log1p(jnp.exp(-jnp.abs(v)))


def split3(v):
    a = v.astype(bf16)
    w = v - a.astype(f32)
    b = w.astype(bf16)
    return jnp.concatenate([a, b, (w - b.astype(f32)).astype(bf16)], axis=0)


def merge3(v):
    return v[0:8] + v[8:16] + v[16:24]


def tri_low():
    i = lax.broadcasted_iota(jnp.int32, (SPAN, SPAN), 0)
    j = lax.broadcasted_iota(jnp.int32, (SPAN, SPAN), 1)
    return (i >= j).astype(bf16)


def decay_terms(b, offs, da):
    first = b * SPAN
    row = first + lax.broadcasted_iota(jnp.int32, (1, SPAN), 1)
    col = first + lax.broadcasted_iota(jnp.int32, (SPAN, 1), 0)

    def begin(pos):
        at = jnp.zeros_like(pos)
        for o in offs[1:]:
            at = jnp.where(pos >= o, o, at)
        return at

    beg_r, beg_c = begin(row), begin(col)
    l_row = merge3(nt(split3(da), tri_low()))
    l_col = l_row.T
    last = l_row[:, SPAN - 1 : SPAN]
    end_b = jnp.max(beg_r, axis=1, keepdims=True)
    e = jnp.where(beg_r < first, jnp.exp(l_row), 0.0)
    we = jnp.where(beg_r == end_b, jnp.exp(last - l_row), 0.0)
    kept = jnp.where(end_b < first, jnp.exp(last), 0.0)
    mask = jnp.where((beg_r == beg_c) & (row <= col), 1.0, 0.0)
    return l_row, l_col, e, we, kept, mask, row - beg_r


def wide(ref, k, rows):
    w = ref[k, rows, :]
    return jnp.concatenate([w, w], axis=1)


def fold(v):
    return v[:, 0:128] + v[:, 128:256]


def conv_forward(cur, tail, pref, rows, places):
    win = jnp.concatenate([tail, cur], axis=1)
    u = wide(pref, 3, rows) * cur + wide(pref, 4, rows)
    for s in (1, 2, 3):
        back = jnp.where(places >= s, pltpu.roll(win, s, 1)[:, 128:], 0.0)
        u = u + wide(pref, 3 - s, rows) * back
    return u


def conv_backward(R, raw, du, pref, acc, head, rows, base, tok, m):
    out = wide(pref, 3, rows) * du
    acc[4, rows, :] += fold(du)
    acc[3, rows, :] += fold(du * raw)
    for s in (1, 2, 3):
        w = du * m[s]
        win = jnp.concatenate([w, head[s - 1, rows, :]], axis=1)
        sh = pltpu.roll(win, SPAN + 128 - s, 1)[:, 0:SPAN]
        head[s - 1, rows, :] = w[:, 0:128]
        out = out + wide(pref, 3 - s, rows) * sh
        acc[3 - s, rows, :] += fold(sh * raw)
    R.dcat[base + rows.start : base + rows.stop, tok] = out.astype(bf16)


def scan_block(b, R, offs, C, H):
    p = C // H
    tok = aligned(b * SPAN, SPAN)
    R.pr[...] = nt(R.wcat[C:, :], R.hn[tok, :])
    R.xr[:, tok] = R.pr[0:C, :].astype(bf16)
    R.bcr[:, tok] = R.pr[C : C + BC, :].astype(bf16)
    dr = R.pr[C + BC : C + BC + 8, :] + R.ph[:, 0:1]
    R.dr[:, tok] = dr
    dt = softplus(dr)
    l_row, l_col, e, we, kept, mask, places = decay_terms(b, offs, dt * R.ph[:, 1:2])
    bcr = R.pr[C : C + BC, :]
    u = conv_forward(bcr, R.tail_bc[...], R.pbc, slice(0, BC), places).astype(bf16)
    R.tail_bc[...] = bcr[:, 128:]
    R.ubc[:, tok] = u
    u = u.astype(f32)
    bc = (u * jax.nn.sigmoid(u)).astype(bf16)
    bt, ct = bc[0:STATE, :], bc[STATE:BC, :]
    R.gm[...] = tn(ct, bt) * mask
    for h in range(H):
        rows = slice(h * p, (h + 1) * p)
        hh = slice(h, h + 1)
        xr = R.pr[rows, :]
        u = conv_forward(xr, R.tail_x[rows, :], R.px, rows, places).astype(bf16)
        R.tail_x[rows, :] = xr[:, 128:]
        R.ux[rows, tok] = u
        u = u.astype(f32)
        xd = u * jax.nn.sigmoid(u) * dt[hh, :]
        d = jnp.exp(jnp.minimum(l_col[:, hh] - l_row[hh, :], 0.0))
        mix = (d * R.gm[...]).astype(bf16)
        st = R.state[rows, :]
        stb = st.astype(bf16)
        R.states[b, rows, :] = stb
        R.y[rows, tok] = nt(xd.astype(bf16), mix) + nn(stb, ct) * e[hh, :]
        R.state[rows, :] = kept[hh, :] * st + nt((xd * we[hh, :]).astype(bf16), bt)


def gate_block(b, R, C, H):
    p = C // H
    tok = aligned(b * SPAN, SPAN)
    R.z[:, tok] = nt(R.wcat[0:C, :], R.hn[tok, :]).astype(bf16)
    sq = jnp.zeros((1, SPAN), f32)
    for h in range(H):
        rows = slice(h * p, (h + 1) * p)
        u = R.ux[rows, tok].astype(f32)
        zz = R.z[rows, tok].astype(f32)
        yf = R.y[rows, tok] + wide(R.px, 6, rows) * (u * jax.nn.sigmoid(u))
        gy = yf * (zz * jax.nn.sigmoid(zz))
        sq = sq + jnp.sum(gy * gy, axis=0, keepdims=True)
        R.gg[rows, tok] = (gy * wide(R.px, 5, rows)).astype(bf16)
    R.sums[0, pl.ds(b, 1), :] = sq


def gate_back_block(b, R, C, H, inner):
    p = C // H
    tok = aligned(b * SPAN, SPAN)
    r = lax.rsqrt(R.tot[0, pl.ds(b, 1), :] / inner + EPS)
    rs = r * r * R.tot[1, pl.ds(b, 1), :] / inner
    for h in range(H):
        rows = slice(h * p, (h + 1) * p)
        u = R.ux[rows, tok].astype(f32)
        x = u * jax.nn.sigmoid(u)
        zz = R.z[rows, tok].astype(f32)
        sz = jax.nn.sigmoid(zz)
        gate = zz * sz
        yf = R.y[rows, tok] + wide(R.px, 6, rows) * x
        gy = yf * gate
        dyn = R.dyn[rows, tok].astype(f32)
        R.accx[5, rows, :] += fold(dyn * (gy * r))
        dgy = (r * wide(R.px, 5, rows)) * dyn - gy * rs
        R.dcat[rows, tok] = (dgy * yf * (sz + gate * (1.0 - sz))).astype(bf16)
        dy = dgy * gate
        R.accx[6, rows, :] += fold(dy * x)
        R.dyn[rows, tok] = dy.astype(bf16)


def bwd_block(b, R, offs, C, H):
    p = C // H
    tok = aligned(b * SPAN, SPAN)
    v = R.dr[:, tok]
    dt = softplus(v)
    rate = R.ph[:, 1:2]
    l_row, l_col, e, we, kept, mask, places = decay_terms(b, offs, dt * rate)
    ubc = R.ubc[:, tok].astype(f32)
    sg = jax.nn.sigmoid(ubc)
    bc = (ubc * sg).astype(bf16)
    bt, ct = bc[0:STATE, :], bc[STATE:BC, :]
    R.gm[...] = tn(ct, bt) * mask
    m = [None] + [jnp.where(places >= s, 1.0, 0.0) for s in (1, 2, 3)]
    decays, directs, ends = [], [], []
    for h in range(H):
        rows = slice(h * p, (h + 1) * p)
        hh = slice(h, h + 1)
        u = R.ux[rows, tok].astype(f32)
        sx = jax.nn.sigmoid(u)
        x = u * sx
        y = R.y[rows, tok]
        dyb = R.dyn[rows, tok]
        dy = dyb.astype(f32)
        xd = x * dt[hh, :]
        xdb = xd.astype(bf16)
        d = jnp.exp(jnp.minimum(l_col[:, hh] - l_row[hh, :], 0.0))
        mix = (d * R.gm[...]).astype(bf16)
        vin = nn(dyb, mix)
        dm = tn(dyb, xdb) * d
        if h == 0:
            R.dg[...] = dm
        else:
            R.dg[...] += dm
        stb = R.states[b, rows, :]
        lam = R.state[rows, :]
        lamb = lam.astype(bf16)
        lb = nn(lamb, bt) * we[hh, :]
        vt = vin + lb
        xlow = xdb.astype(f32)
        decays.append(jnp.sum(dy * y - xlow * vt, axis=0, keepdims=True))
        directs.append(jnp.sum(x * vt, axis=0, keepdims=True))
        through = jnp.sum(lam * stb.astype(f32), axis=0, keepdims=True) * kept[hh, :]
        ends.append(
            jnp.sum(xlow * lb, axis=0, keepdims=True)
            + jnp.concatenate([through, jnp.zeros((1, SPAN - STATE), f32)], axis=1)
        )
        edy = (dy * e[hh, :]).astype(bf16)
        R.edy[rows, :] = edy
        R.wxd[rows, :] = (xd * we[hh, :]).astype(bf16)
        R.lamb[rows, :] = lamb
        R.state[rows, :] = kept[hh, :] * lam + nt(edy, ct)
        dx = dt[hh, :] * vt + wide(R.px, 6, rows) * dy
        du = dx * (sx + x * (1.0 - sx))
        conv_backward(R, R.xr[rows, tok].astype(f32), du, R.px, R.accx, R.head_x, rows, C, tok, m)
    dgm = (R.dg[...] * mask).astype(bf16)
    dct = nt(bt, dgm) + tn(R.states[b], R.edy[...])
    dbt = nn(ct, dgm) + tn(R.lamb[...], R.wxd[...])
    du = jnp.concatenate([dbt, dct], axis=0) * (sg + ubc * sg * (1.0 - sg))
    conv_backward(
        R, R.bcr[:, tok].astype(f32), du, R.pbc, R.accbc, R.head_bc, slice(0, BC), 2 * C, tok, m
    )
    pad = [jnp.zeros((8 - H, SPAN), f32)]
    end = jnp.sum(jnp.concatenate(ends + pad, axis=0), axis=1, keepdims=True)
    g = merge3(nn(split3(jnp.concatenate(decays + pad, axis=0)), tri_low())) + end
    ddr = (g * rate + jnp.concatenate(directs + pad, axis=0)) * jax.nn.sigmoid(v)
    R.acch[0] += ddr
    R.acch[1] += g * dt * rate
    R.dcat[2 * C + BC : 2 * C + BC + 16, tok] = jnp.concatenate(
        [ddr, jnp.zeros((8, SPAN), f32)], axis=0
    ).astype(bf16)


def remote(src, dst, send, recv, device):
    return pltpu.make_async_remote_copy(
        src_ref=src, dst_ref=dst, send_sem=send, recv_sem=recv, device_id=device, device_id_type=MESH
    )


class Place:
    def __init__(self, n):
        self.n = n
        self.dp, self.row, self.col = (lax.axis_index(a) for a in ("dp", "row", "col"))
        self.x, self.c, self.y = self.row // 2, self.row % 2, self.col
        self.q = self.index(self.x, self.c, self.y)
        self.mate = (self.dp, self.x * 2 + 1 - self.c, self.y)
        self.xn = (self.dp, (1 - self.x) * 2 + self.c, self.y)
        self.yn = (self.dp, self.row, 1 - self.y)
        self.diag = (self.dp, (1 - self.x) * 2 + self.c, 1 - self.y)

    def index(self, x, c, y):
        return (x * 2 + c) * 2 + y

    def plane(self, d):
        k = (self.q + d) % 8
        return k, (self.dp, k // 2, k % 2)

    def line(self, d):
        k = (self.dp + d) % self.n
        return k, (k, self.row, self.col)

    def right(self):
        return (self.dp + 1, self.row, self.col)

    def left(self):
        return (self.dp - 1, self.row, self.col)


class PlaneGather:
    def __init__(self, me, buf, send, recv):
        self.me, self.buf, self.send, self.recv = me, buf, send, recv
        x, c, y = me.x, me.c, me.y
        own = lambda cc: (
            me.index(x, cc, y),
            me.index(1 - x, cc, y),
            me.index(x, cc, 1 - y),
            me.index(1 - x, cc, 1 - y),
        )
        self.q, self.qx, self.qy, self.qd = own(c)
        self.mq, self.mx, self.my, self.md = own(1 - c)

    def at(self, k, half):
        if half is None:
            return self.buf.at[aligned(k * SPAN, SPAN), :]
        return self.buf.at[aligned(k * SPAN + half * HALF, HALF), :]

    def copy(self, i, k, half, device):
        region = self.at(k, half)
        return remote(region, region, self.send.at[i], self.recv.at[i], device)

    def wait(self, i, k, half):
        self.copy(i, k, half, self.me.mate).wait_recv()

    def start(self):
        me = self.me
        self.copy(0, self.q, 0, me.xn).start()
        self.copy(3, self.q, 1, me.yn).start()
        self.copy(1, self.q, 1, me.xn).start()
        self.copy(2, self.q, 0, me.yn).start()
        self.copy(6, self.q, None, me.mate).start()

    def step1(self):
        me = self.me
        self.wait(0, self.qx, 0)
        self.copy(4, self.qx, 0, me.yn).start()
        self.copy(7, self.qx, 0, me.mate).start()
        self.wait(3, self.qy, 1)
        self.copy(5, self.qy, 1, me.xn).start()
        self.copy(10, self.qy, 1, me.mate).start()

    def step2(self):
        me = self.me
        self.wait(1, self.qx, 1)
        self.copy(8, self.qx, 1, me.mate).start()
        self.wait(2, self.qy, 0)
        self.copy(9, self.qy, 0, me.mate).start()

    def step3(self):
        me = self.me
        self.wait(4, self.qd, 0)
        self.copy(11, self.qd, 0, me.mate).start()
        self.wait(5, self.qd, 1)
        self.copy(12, self.qd, 1, me.mate).start()

    def step4(self):
        self.wait(6, self.mq, None)
        self.wait(7, self.mx, 0)
        self.wait(8, self.mx, 1)
        self.wait(9, self.my, 0)
        self.wait(10, self.my, 1)
        self.wait(11, self.md, 0)
        self.wait(12, self.md, 1)
        for i in range(13):
            self.copy(i, self.q, None if i == 6 else 0, self.me.mate).wait_send()


def both(*conds):
    out = conds[0]
    for c in conds[1:]:
        out = jnp.logical_and(out, c)
    return out


class LineGather:
    def __init__(self, me, at, send, recv):
        self.me, self.at, self.send, self.recv = me, at, send, recv

    def copy(self, way, s, k):
        device = self.me.right() if way == 0 else self.me.left()
        return remote(self.at(k), self.at(k), self.send.at[way, s], self.recv.at[way, s], device)

    def start(self):
        me = self.me

        @pl.when(me.dp < me.n - 1)
        def _():
            self.copy(0, 0, me.dp).start()

        @pl.when(me.dp > 0)
        def _():
            self.copy(1, 0, me.dp).start()

    def step(self, s):
        me = self.me
        k = me.dp - 1 - s
        j = me.dp + 1 + s

        @pl.when(k >= 0)
        def _():
            self.copy(0, s, k).wait_recv()

        @pl.when(j <= me.n - 1)
        def _():
            self.copy(1, s, j).wait_recv()

        @pl.when(both(me.dp < me.n - 1, me.dp - s >= 0))
        def _():
            self.copy(0, s, me.dp).wait_send()

        @pl.when(both(me.dp > 0, me.dp + s <= me.n - 1))
        def _():
            self.copy(1, s, me.dp).wait_send()

        @pl.when(both(k >= 0, me.dp < me.n - 1, s < me.n - 2))
        def _():
            self.copy(0, s + 1, k).start()

        @pl.when(both(j <= me.n - 1, me.dp > 0, s < me.n - 2))
        def _():
            self.copy(1, s + 1, j).start()


class LineScatter:
    def __init__(self, me, src, slot, send, recv):
        self.me, self.src, self.slot, self.send, self.recv = me, src, slot, send, recv

    def copy(self, way, s, what, to):
        (a, i), (b, j) = what, to
        device = self.me.right() if way == 0 else self.me.left()
        return remote(a.at[i], b.at[j], self.send.at[way, s], self.recv.at[way, s], device)

    def got(self, way, s, slot):
        self.copy(way, s, slot, slot).wait_recv()

    def add(self, k):
        (a, i), (b, j) = self.slot(k), self.src(k)
        a[i] = (a[i].astype(f32) + b[j].astype(f32)).astype(bf16)

    def moves(self, t):
        me, n = self.me, self.me.n
        s, v = t - me.dp, t - (n - 1 - me.dp)
        return both(s >= 0, n - 1 - s > me.dp), s, n - 1 - s, both(v >= 0, v < me.dp), v, v

    def slot_step(self, t):
        me, n = self.me, self.me.n
        to_right, s, k, to_left, v, j = self.moves(t)

        @pl.when(both(to_right, me.dp > 0))
        def _():
            self.got(0, s, self.slot(k))
            self.add(k)
            self.copy(0, s, self.slot(k), self.slot(k)).start()

        @pl.when(both(to_right, me.dp == 0))
        def _():
            self.copy(0, s, self.src(k), self.slot(k)).start()

        to = self.slot(jnp.where(j == me.dp - 1, n, j))

        @pl.when(both(to_left, me.dp < n - 1))
        def _():
            self.got(1, v, self.slot(j))
            self.add(j)
            self.copy(1, v, self.slot(j), to).start()

        @pl.when(both(to_left, me.dp == n - 1))
        def _():
            self.copy(1, v, self.src(j), to).start()

    def total(self, put):
        me, n = self.me, self.me.n
        a, i = self.src(me.dp)
        put(a[i].astype(f32), True)

        @pl.when(me.dp > 0)
        def _():
            b, j = self.slot(me.dp)
            self.got(0, n - 1 - me.dp, (b, j))
            put(b[j].astype(f32), False)

        @pl.when(me.dp < n - 1)
        def _():
            b, j = self.slot(n)
            self.got(1, me.dp, (b, j))
            put(b[j].astype(f32), False)

    def finish(self, t):
        to_right, s, k, to_left, v, j = self.moves(t)

        @pl.when(to_right)
        def _():
            self.copy(0, s, self.src(0), self.slot(0)).wait_send()

        @pl.when(to_left)
        def _():
            self.copy(1, v, self.src(0), self.slot(0)).wait_send()


class PlaneScatter:
    def __init__(self, me, R, send, recv, part, credit):
        self.me, self.R, self.send, self.recv, self.part, self.credit = me, R, send, recv, part, credit
        x, y = me.x, me.y
        self.jo, self.jx, self.jy, self.jd = x * 2 + y, (1 - x) * 2 + y, x * 2 + 1 - y, (1 - x) * 2 + 1 - y

    def copy(self, i, src, dst, device):
        return remote(src, dst, self.send.at[i], self.recv.at[i], device)

    def first(self):
        me, R = self.me, self.R
        if self.credit:
            pl.semaphore_wait(R.free.at[0], 1)

        @pl.loop(0, 4)
        def _(j):
            k = me.index(j // 2, 1 - me.c, j % 2)

            @pl.when(j >= 2)
            def _():
                self.copy(j - 2, R.sb.at[j % 2], R.rb.at[j - 2], me.mate).wait_send()

            R.sb[j % 2, 0] = self.part(k, 0).astype(bf16)
            R.sb[j % 2, 1] = self.part(k, 1).astype(bf16)
            self.copy(j, R.sb.at[j % 2], R.rb.at[j], me.mate).start()

    def second(self):
        me, R = self.me, self.R
        if self.credit:
            pl.semaphore_wait(R.free.at[1], 1)
            pl.semaphore_wait(R.free.at[2], 1)

        @pl.loop(0, 4)
        def _(t):
            dx, dy = 1 - t // 2, 1 - t % 2
            xx = me.x + dx * (1 - 2 * me.x)
            yy = me.y + dy * (1 - 2 * me.y)
            j = xx * 2 + yy
            k = me.index(xx, me.c, yy)
            self.copy(j, R.sb.at[0], R.rb.at[j], me.mate).wait_recv()
            R.rb[j, 0] = (self.part(k, 0) + R.rb[j, 0].astype(f32)).astype(bf16)
            R.rb[j, 1] = (self.part(k, 1) + R.rb[j, 1].astype(f32)).astype(bf16)

            @pl.when(t == 0)
            def _():
                self.copy(4, R.rb.at[self.jd, 0], R.da, me.xn).start()
                self.copy(5, R.rb.at[self.jd, 1], R.db, me.yn).start()

            @pl.when(t == 1)
            def _():
                self.copy(6, R.rb.at[self.jx, 0], R.fx.at[0], me.xn).start()

            @pl.when(t == 2)
            def _():
                self.copy(9, R.rb.at[self.jy, 1], R.fy.at[1], me.yn).start()

    def relay(self):
        me, R = self.me, self.R
        self.copy(4, R.da, R.da, me.xn).wait_recv()
        R.rb[self.jy, 0] = (R.rb[self.jy, 0].astype(f32) + R.da[...].astype(f32)).astype(bf16)
        self.copy(8, R.rb.at[self.jy, 0], R.fy.at[0], me.yn).start()
        self.copy(5, R.db, R.db, me.yn).wait_recv()
        R.rb[self.jx, 1] = (R.rb[self.jx, 1].astype(f32) + R.db[...].astype(f32)).astype(bf16)
        self.copy(7, R.rb.at[self.jx, 1], R.fx.at[1], me.xn).start()

    def total(self, put):
        me, R = self.me, self.R
        for half in (0, 1):
            self.copy(6 + half, R.fx.at[half], R.fx.at[half], me.xn).wait_recv()
            self.copy(8 + half, R.fy.at[half], R.fy.at[half], me.yn).wait_recv()
            steps = R.da.shape[0] // 128

            @pl.loop(0, steps)
            def _(i):
                rows = aligned(i * 128, 128)
                v = R.rb[self.jo, half, rows, :].astype(f32)
                put(half * steps + i, v + R.fx[half, rows, :].astype(f32) + R.fy[half, rows, :].astype(f32))

    def finish(self, release):
        me, R = self.me, self.R
        for i in (2, 3):
            self.copy(i, R.sb.at[i % 2], R.rb.at[i], me.mate).wait_send()
        for i in range(4, 10):
            self.copy(i, R.da, R.db, me.mate).wait_send()
        if release:
            for i, device in enumerate((me.mate, me.xn, me.yn)):
                pl.semaphore_signal(R.free.at[i], 1, device_id=device, device_id_type=MESH)


def stepped(n, *fns):
    if n <= 4:
        return [lambda s=s: [f(s) for f in fns] for s in range(n - 1)]

    def every():
        @pl.loop(0, n - 1)
        def _(s):
            for f in fns:
                f(s)

    return [every] + [lambda: None] * 2


def kernel(names, n, C, H, *refs):
    R = types.SimpleNamespace(**dict(zip(names, refs)))
    me = Place(n)
    T, D = R.hn.shape
    inner = R.gate.shape[0]
    heads = R.skip.shape[0]
    nb = T // SPAN
    DS = D // n
    dp = me.dp
    rows = 2 * C + BC + 16
    dt_rows = slice(2 * C + BC, rows)
    share = lambda k: pl.ds(pl.multiple_of(k * DS, 16), DS)
    dhalf = lambda h: slice(h * (D // 2), (h + 1) * (D // 2))
    half = aligned(2 * C + me.c * 128, 128)
    other = aligned(2 * C + (1 - me.c) * 128, 128)

    def over(length):
        def run(f):
            pl.loop(0, length)(f)

        return run

    def beside(i, polls):
        for k, fns in polls.items():

            @pl.when(i == k)
            def _():
                for f in fns:
                    f()

    stage = lambda a, z: R.y.at[0:DS, a:z]
    arriving = [
        pltpu.make_async_copy(src, dst, R.loc.at[i])
        for i, (src, dst) in enumerate(
            (
                (R.wx, stage(C, 2 * C)),
                (R.wbc, stage(2 * C, 2 * C + BC)),
                (R.wz, stage(0, C)),
                (R.gcot, R.cot.at[aligned(me.q * SPAN, SPAN), :]),
            )
        )
    ]
    for copy in arriving:
        copy.start()
    barrier = pltpu.get_barrier_semaphore()
    for d in range(1, 8):
        pl.semaphore_signal(barrier, 1, device_id=me.plane(d)[1], device_id_type=MESH)
    for d in range(1, n):
        pl.semaphore_signal(barrier, 1, device_id=me.line(d)[1], device_id_type=MESH)
    R.gains[...] = R.gain[...].reshape(1, D)

    @over(SPAN // 32)
    def _(i):
        u = R.hid[aligned(i * 32, 32), :].astype(f32)
        qn = lax.rsqrt(jnp.mean(u * u, axis=1, keepdims=True) + EPS)
        R.hn[aligned(me.q * SPAN + i * 32, 32), :] = (u * qn * R.gains[...]).astype(bf16)

    for copy in arriving[:2]:
        copy.wait()
    R.wd[share(dp), C : 2 * C] = R.y[0:DS, C : 2 * C].astype(bf16)
    R.wd[share(dp), half] = R.y[0:DS, half].astype(bf16)
    R.wdt[dp] = jnp.concatenate([R.w_dt[...], jnp.zeros((DS, 128 - H), f32)], axis=1).T[0:16, :].astype(bf16)
    pl.semaphore_wait(barrier, 7 + n - 1)

    tokens = PlaneGather(me, R.hn, R.ag_s.at[0], R.ag_r.at[0])
    cots = PlaneGather(me, R.cot, R.ag_s.at[1], R.ag_r.at[1])
    places = (
        lambda k: R.wd.at[share(k), C : 2 * C],
        lambda k: R.wd.at[share(k), half],
        lambda k: R.wdt.at[k],
        lambda k: R.wd.at[share(k), 0:C],
        lambda k: R.wot.at[share(k), :],
    )
    gathers = [LineGather(me, at, R.za_s.at[i], R.za_r.at[i]) for i, at in enumerate(places)]
    z_gather, wo_gather = gathers[3:]
    tokens.start()
    for g in gathers[:3]:
        g.start()

    for copy in arriving[2:]:
        copy.wait()
    R.wd[share(dp), 0:C] = R.y[0:DS, 0:C].astype(bf16)
    R.wot[share(dp), :] = R.wo[...].T.astype(bf16)
    own = aligned(me.q * C, C)
    taps = [R.conv_x[:, own]]
    for v in (R.conv_xb, R.gate):
        R.row[...] = v[...].reshape(1, inner)
        taps.append(R.row[:, own])
    taps = jnp.concatenate(taps + [jnp.zeros((2, C), f32)], axis=0).T
    chan = lax.broadcasted_iota(jnp.int32, (C, heads), 0) // (C // H) + me.q * H
    pick = chan == lax.broadcasted_iota(jnp.int32, (C, heads), 1)
    skips = jnp.sum(jnp.where(pick, R.skip[...].reshape(1, heads), 0.0), axis=1, keepdims=True)
    for k in range(6):
        R.px[k] = jnp.broadcast_to(taps[:, k : k + 1], (C, 128))
    R.px[6] = jnp.broadcast_to(skips, (C, 128))
    taps = jnp.concatenate([R.conv_bc[...], R.conv_bcb[...].reshape(1, BC), jnp.zeros((3, BC), f32)], axis=0).T
    for k in range(5):
        R.pbc[k] = jnp.broadcast_to(taps[:, k : k + 1], (BC, 128))
    head = lax.broadcasted_iota(jnp.int32, (8, heads), 0)
    pick = (head + me.q * H == lax.broadcasted_iota(jnp.int32, (8, heads), 1)) & (head < H)
    R.ph[:, 0:1] = jnp.sum(jnp.where(pick, R.dt_bias[...].reshape(1, heads), 0.0), axis=1, keepdims=True)
    R.ph[:, 1:2] = jnp.sum(
        jnp.where(pick, -jnp.exp(R.a_log[...].reshape(1, heads)), 0.0), axis=1, keepdims=True
    )
    for a in (R.tail_bc, R.tail_x, R.state, R.head_x, R.head_bc, R.accx, R.accbc, R.acch, R.sv):
        a[...] = jnp.zeros_like(a)
    offs = [0]
    for k in range(R.perm.shape[0] - 1):
        offs.append(offs[-1] + R.lengths[R.perm[k]])

    def line(*fns):
        if n <= 4:
            return [lambda s=s: [f(s) for f in fns] for s in range(n - 1)] + [lambda: None] * (4 - n)

        def every():
            @over(n - 1)
            def _(s):
                for f in fns:
                    f(s)

        return [every] + [lambda: None] * 2

    def prepare(a, z):
        for k in range(a, z, 128):
            R.wcat[k : k + 128, :] = R.wd[:, k : k + 128].T

    steps = line(*[g.step for g in gathers[:3]])
    tokens.step1()
    steps[0]()
    tokens.step2()
    steps[1]()
    tokens.step3()
    cots.start()
    steps[2]()
    z_gather.start()
    bc_swap = remote(R.wd.at[:, half], R.wd.at[:, half], R.mate_s.at[0], R.mate_r.at[0], me.mate)
    bc_swap.start()
    prepare(C, 2 * C)
    for k in range(n):
        R.wcat[dt_rows, k * DS : (k + 1) * DS] = R.wdt[k]
    pad = jnp.zeros((112, D), bf16)
    R.wd[:, 2 * C + BC : 2 * C + BC + 128] = jnp.concatenate([R.wcat[dt_rows, :], pad], axis=0).T
    remote(R.wd.at[:, other], R.wd.at[:, other], R.mate_s.at[0], R.mate_r.at[0], me.mate).wait_recv()
    bc_swap.wait_send()
    prepare(2 * C, 2 * C + BC)
    tokens.step4()

    steps = line(z_gather.step)
    polls = {1: [steps[0]], 2: [cots.step1], 4: [steps[1]], 5: [cots.step2], 6: [steps[2], wo_gather.start]}

    @over(nb)
    def _(b):
        scan_block(b, R, offs, C, H)
        beside(b, polls)

    prepare(0, C)

    @over(nb)
    def _(b):
        gate_block(b, R, C, H)

    def share_sums(i):
        for d in range(1, 8):
            k, device = me.plane(d)
            remote(R.sums.at[i], R.sslot.at[i, me.q], R.sum_s.at[i, k], R.sum_r.at[i, me.q], device).start()
        R.sslot[i, me.q] = R.sums[i]

    def total_sums(i):
        for d in range(1, 8):
            k, device = me.plane(d)
            remote(R.sums.at[i], R.sslot.at[i, k], R.sum_s.at[i, k], R.sum_r.at[i, k], device).wait()
        total = R.sslot[i, 0]
        for k in range(1, 8):
            total = total + R.sslot[i, k]
        R.tot[i] = total

    share_sums(0)
    steps = line(wo_gather.step)
    steps[0]()
    cots.step3()
    cots.step4()
    total_sums(0)

    @over(nb)
    def _(b):
        tok = aligned(b * SPAN, SPAN)
        r = lax.rsqrt(R.tot[0, pl.ds(b, 1), :] / inner + EPS)
        R.gg[:, tok] = (R.gg[:, tok].astype(f32) * r).astype(bf16)

    @over(D // 256)
    def _(i):
        some = aligned(i * 256, 256)
        R.won[some, :] = nn(R.gg[...], R.cot[:, some]).astype(bf16).T

    steps[1]()

    def scatter(i, src, lanes):
        slot = lambda k: (R.cot, (share(k), slice(*lanes)))
        return LineScatter(me, src, slot, R.zr_s.at[i], R.zr_r.at[i])

    wo_sum = scatter(0, lambda k: (R.won, (share(k), slice(0, C))), (2 * C + 128, 3 * C + 128))
    x_sum = scatter(1, lambda k: (R.wd, (share(k), slice(C, 2 * C))), (C, 2 * C))
    z_sum = scatter(2, lambda k: (R.wot, (share(k), slice(0, C))), (0, C))
    bc_sum = scatter(3, lambda k: (R.wd, (share(k), half)), (2 * C, 2 * C + 128))
    dt_sum = LineScatter(
        me, lambda k: (R.gdt, (k,)), lambda k: (R.rdt, (k,)), R.zr_s.at[4], R.zr_r.at[4]
    )
    steps[2]()
    for k in range(0, D, 256):
        R.wout[:, k : k + 256] = R.wot[k : k + 256, :].T

    @over(nb)
    def _(b):
        tok = aligned(b * SPAN, SPAN)
        dyn = nt(R.wout[...], R.cot[tok, :])
        R.dyn[:, tok] = dyn.astype(bf16)
        R.sums[1, pl.ds(b, 1), :] = jnp.sum(dyn * R.gg[:, tok].astype(f32), axis=0, keepdims=True)

    share_sums(1)

    @pl.when(dp < n - 1)
    def _():
        pl.semaphore_signal(R.free.at[3], 1, device_id=me.right(), device_id_type=MESH)

    @pl.when(dp > 0)
    def _():
        pl.semaphore_signal(R.free.at[4], 1, device_id=me.left(), device_id_type=MESH)

    mixed = PlaneScatter(
        me,
        R,
        R.rs_s.at[0],
        R.rs_r.at[0],
        lambda k, h: nn(R.wot[dhalf(h), :], R.gg[:, aligned(k * SPAN, SPAN)]),
        False,
    )
    mixed.first()

    @pl.when(dp > 0)
    def _():
        pl.semaphore_wait(R.free.at[3], 1)

    @pl.when(dp < n - 1)
    def _():
        pl.semaphore_wait(R.free.at[4], 1)

    wo_steps = line(wo_sum.slot_step)
    wo_steps[0]()
    mixed.second()
    total_sums(1)

    @over(nb)
    def _(b):
        gate_back_block(b, R, C, H, inner)

    def weight_grad(a, z, dst, at):
        @over(D // 256)
        def _(i):
            some = aligned(i * 256, 256)
            g = nn(R.dcat[a:z, :], R.hn[:, some])
            R.ng[:, some] += jnp.sum(g * R.wcat[a:z, some].astype(f32), axis=0, keepdims=True)
            g = g.astype(bf16)
            if z - a > 256:
                R.gdt_all[:, some] = g[z - a - 16 : z - a]
            w = min(z - a, 256)
            dst[some, at : at + w] = g[0:w].T

    R.ng[...] = jnp.zeros_like(R.ng)
    weight_grad(0, 256, R.wot, 0)
    weight_grad(256, C, R.wot, 256)
    wo_steps[1]()

    def put(ref):
        def f(v, new):
            if new:
                ref[...] = v
            else:
                ref[...] += v

        return f

    out_copy = pltpu.make_async_copy(R.wout.at[0:SPAN, :], R.block_out, R.loc.at[5])

    def finish_mixed():
        def put(k, v):
            cols = aligned(k * 128, 128)
            R.wout[0:SPAN, cols] = (R.hid[:, cols].astype(f32) + v.T).astype(bf16)

        mixed.total(put)
        out_copy.start()
        mixed.finish(True)

    R.state[...] = jnp.zeros_like(R.state)
    z_steps = line(z_sum.slot_step)
    polls = {
        0: [mixed.relay],
        1: [wo_steps[2], z_steps[0]],
        4: [z_steps[1], finish_mixed],
        7: [z_steps[2]],
    }

    @over(nb)
    def _(i):
        bwd_block(nb - 1 - i, R, offs, C, H)
        beside(i, polls)

    dhn = PlaneScatter(
        me,
        R,
        R.rs_s.at[1],
        R.rs_r.at[1],
        lambda k, h: nn(R.wd[dhalf(h), 0:rows], R.dcat[:, aligned(k * SPAN, SPAN)]),
        True,
    )
    dhn.first()
    dhn.second()

    weight_grad(2 * C - 256, 2 * C, R.wd, 2 * C - 256)
    weight_grad(C, 2 * C - 256, R.wd, C)
    x_steps = line(x_sum.slot_step)
    x_steps[0]()
    weight_grad(2 * C, rows, R.wd, 2 * C)
    for k in range(n):
        R.gdt[k] = R.gdt_all[:, k * DS : (k + 1) * DS]
    bx = R.cot.at[0:D, 3 * C + 128 : 3 * C + 256]
    bc_pair = remote(R.wd.at[:, other], bx, R.mate_s.at[1], R.mate_r.at[1], me.mate)
    bc_pair.start()
    dhn.relay()

    ax = [jnp.sum(R.accx[k], axis=1, keepdims=True) for k in range(7)]
    ab = [jnp.sum(R.accbc[k], axis=1, keepdims=True) for k in range(5)]
    ah = [jnp.sum(R.acch[k], axis=1, keepdims=True) for k in range(2)]
    p = C // H
    ah += [jnp.sum(ax[6][h * p : (h + 1) * p], axis=0, keepdims=True) for h in range(H)]
    ah = jnp.concatenate(ah + [jnp.zeros((8 - H, 1), f32)], axis=0)
    R.sv[0:8, :] = jnp.concatenate(ax[:6] + [jnp.zeros((C, 2), f32)], axis=1).T
    R.sv[6:7, 0:128] = jnp.concatenate(
        [jnp.broadcast_to(ah, (24, 128)), jnp.zeros((104, 128), f32)], axis=0
    ).T[0:1, :]
    R.sv[8:16, 0:BC] = jnp.concatenate(ab + [jnp.zeros((BC, 3), f32)], axis=1).T
    ng = R.ng[...] / R.gains[...]
    for k in range(D // C):
        R.sv[16 + k : 17 + k, :] = ng[:, k * C : (k + 1) * C]
    for d in range(1, n):
        k, device = me.line(d)
        remote(R.sv, R.lslot.at[dp], R.ls_s.at[k], R.ls_r.at[dp], device).start()
    R.lslot[dp] = R.sv[...]
    x_steps[1]()
    bc_pair.wait()
    R.wd[:, half] = (R.wd[:, half].astype(f32) + bx[...].astype(f32)).astype(bf16)
    bc_steps = line(bc_sum.slot_step, dt_sum.slot_step)
    bc_steps[0]()
    for d in range(1, n):
        k, device = me.line(d)
        remote(R.sv, R.lslot.at[k], R.ls_s.at[k], R.ls_r.at[k], device).wait()
    total = R.lslot[0]
    for k in range(1, n):
        total = total + R.lslot[k]
    R.pv[...] = total
    for d in range(1, 8):
        k, device = me.plane(d)
        remote(R.pv, R.small.at[me.q], R.ps_s.at[k], R.ps_r.at[me.q], device).start()
    R.small[me.q] = total
    bc_steps[1]()
    x_steps[2]()
    bc_steps[2]()

    wo_sum.total(put(R.gwo))
    z_sum.total(put(R.gz))
    bc_sum.total(put(R.bsum))
    j = me.x * 2 + me.y
    R.bslot[j] = R.bsum[...].astype(bf16)
    crossing = []
    for i, (device, k) in enumerate(
        ((me.xn, (1 - me.x) * 2 + me.y), (me.yn, me.x * 2 + 1 - me.y), (me.diag, (1 - me.x) * 2 + 1 - me.y))
    ):
        remote(R.bslot.at[j], R.bslot.at[j], R.bc_s.at[i], R.bc_r.at[i], device).start()
        crossing.append(remote(R.bslot.at[k], R.bslot.at[k], R.bc_s.at[i], R.bc_r.at[i], device))
    x_sum.total(put(R.gx))
    dt_sum.total(put(R.gdt_out))
    for c in crossing:
        c.wait()
    v = R.bslot[0].astype(f32)
    for k in range(1, 4):
        v = v + R.bslot[k].astype(f32)
    R.bfin[me.c] = v.astype(bf16)
    bc_last = remote(R.bfin.at[me.c], R.bfin.at[me.c], R.mate_s.at[2], R.mate_r.at[2], me.mate)
    bc_last.start()

    cot_again = pltpu.make_async_copy(R.gcot, R.hn.at[0:SPAN, :], R.loc.at[4])
    cot_again.start()

    def put_dh(k, v):
        R.y[0:SPAN, aligned(k * 128, 128)] = v.T

    dhn.total(put_dh)
    cot_again.wait()

    @over(SPAN // 32)
    def _(i):
        some = aligned(i * 32, 32)
        u = R.hid[some, :].astype(f32)
        qn = lax.rsqrt(jnp.mean(u * u, axis=1, keepdims=True) + EPS)
        w = R.y[some, 0:D] * R.gains[...]
        dot = jnp.sum(w * u, axis=1, keepdims=True) / D
        R.hn[aligned(SPAN + i * 32, 32), :] = (
            R.hn[some, :].astype(f32) + qn * w - u * (qn * qn * qn * dot)
        ).astype(bf16)

    in_copy = pltpu.make_async_copy(R.hn.at[SPAN : 2 * SPAN, :], R.grad_in, R.loc.at[6])
    in_copy.start()
    bc_last.wait_send()
    remote(
        R.bfin.at[1 - me.c], R.bfin.at[1 - me.c], R.mate_s.at[2], R.mate_r.at[2], me.mate
    ).wait_recv()
    R.gbc[:, 0:128] = R.bfin[0].astype(f32)
    R.gbc[:, 128:256] = R.bfin[1].astype(f32)
    for d in range(1, 8):
        k, device = me.plane(d)
        remote(R.pv, R.small.at[k], R.ps_s.at[k], R.ps_r.at[k], device).wait()
    dhn.finish(False)
    for fin in (wo_sum, x_sum, z_sum, bc_sum, dt_sum):
        for s in line(fin.finish):
            s()
    in_copy.wait()
    out_copy.wait()


def unpack(names, C, H, *refs):
    R = types.SimpleNamespace(**dict(zip(names, refs)))
    big = [
        pltpu.make_async_copy(a, b, R.sem.at[i])
        for i, (a, b) in enumerate(
            (
                (R.block_out, R.o_block),
                (R.grad_in, R.o_grad),
                (R.gz, R.o_z),
                (R.gx, R.o_x),
                (R.gbc, R.o_bc),
            )
        )
    ]
    for copy in big:
        copy.start()
    R.o_wo[...] = R.gwo[...].T
    DS = R.gdt_out.shape[1]
    R.o_dt[...] = jnp.concatenate([R.gdt_out[...], jnp.zeros((112, DS), f32)], axis=0).T[:, 0:H]
    row = lambda k: jnp.concatenate([R.small[q, k : k + 1, :] for q in range(8)], axis=1)
    for k in range(KERNEL):
        R.o_cx[k : k + 1, :] = row(k)
    R.o_cxb[...] = row(4).reshape(8 * C)
    R.o_gate[...] = row(5).reshape(8 * C)
    for ref, at in ((R.o_dtb, 0), (R.o_alog, 8), (R.o_skip, 16)):
        v = jnp.concatenate([R.small[q, 6:7, at : at + H] for q in range(8)], axis=1)
        ref[...] = v.reshape(8 * H)
    total = R.small[0, 8:24, :]
    for q in range(1, 8):
        total = total + R.small[q, 8:24, :]
    R.o_cbc[...] = total[0:KERNEL, 0:BC]
    R.o_cbcb[...] = total[4:5, 0:BC].reshape(BC)
    D = R.o_ng.shape[0]
    R.o_ng[...] = jnp.concatenate([total[8 + k : 9 + k, :] for k in range(D // C)], axis=1).reshape(D)
    for copy in big:
        copy.wait()


def shards(
    n,
    hidden_in,
    lengths,
    perm,
    norm_gain,
    w_z,
    w_x,
    w_dt,
    w_bc,
    conv_x,
    conv_x_bias,
    conv_bc,
    conv_bc_bias,
    dt_bias,
    a_log,
    skip_d,
    gate_gain,
    w_out,
    grad_out,
):
    rows, D = hidden_in.shape
    T = rows * 8
    DS, C = w_z.shape
    H = w_dt.shape[1]
    inner = gate_gain.shape[0]
    nb = T // SPAN
    wide_rows = 2 * C + BC + 16
    inputs = dict(
        hid=hidden_in,
        gcot=grad_out,
        wz=w_z,
        wx=w_x,
        wbc=w_bc,
        w_dt=w_dt,
        wo=w_out,
        gain=norm_gain,
        conv_x=conv_x,
        conv_xb=conv_x_bias,
        conv_bc=conv_bc,
        conv_bcb=conv_bc_bias,
        dt_bias=dt_bias,
        a_log=a_log,
        skip=skip_d,
        gate=gate_gain,
        lengths=lengths,
        perm=perm,
    )
    outputs = dict(
        block_out=((rows, D), bf16),
        grad_in=((rows, D), bf16),
        gz=((DS, C), f32),
        gx=((DS, C), f32),
        gbc=((DS, BC), f32),
        gdt_out=((16, DS), f32),
        gwo=((DS, C), f32),
        small=((8, 24, C), f32),
    )
    scratch = dict(
        hn=((T, D), bf16),
        cot=((T, D), bf16),
        wd=((D, 2 * C + BC + 128), bf16),
        wcat=((wide_rows, D), bf16),
        wot=((D, C), bf16),
        wout=((C, D), bf16),
        won=((D, C), bf16),
        wdt=((n, 16, DS), bf16),
        pr=((C + BC + 16, SPAN), f32),
        z=((C, T), bf16),
        xr=((C, T), bf16),
        bcr=((BC, T), bf16),
        ux=((C, T), bf16),
        ubc=((BC, T), bf16),
        dr=((8, T), f32),
        y=((C, T), f32),
        gg=((C, T), bf16),
        dyn=((C, T), bf16),
        dcat=((wide_rows, T), bf16),
        states=((nb, C, STATE), bf16),
        state=((C, STATE), f32),
        gm=((SPAN, SPAN), f32),
        dg=((SPAN, SPAN), f32),
        edy=((C, SPAN), bf16),
        wxd=((C, SPAN), bf16),
        lamb=((C, STATE), bf16),
        tail_x=((C, 128), f32),
        tail_bc=((BC, 128), f32),
        head_x=((3, C, 128), f32),
        head_bc=((3, BC, 128), f32),
        px=((7, C, 128), f32),
        pbc=((5, BC, 128), f32),
        ph=((8, 128), f32),
        row=((1, inner), f32),
        gains=((1, D), f32),
        accx=((7, C, 128), f32),
        accbc=((5, BC, 128), f32),
        acch=((2, 8, SPAN), f32),
        sums=((2, nb, SPAN), f32),
        tot=((2, nb, SPAN), f32),
        sslot=((2, 8, nb, SPAN), f32),
        sb=((2, 2, D // 2, SPAN), bf16),
        rb=((4, 2, D // 2, SPAN), bf16),
        da=((D // 2, SPAN), bf16),
        db=((D // 2, SPAN), bf16),
        fx=((2, D // 2, SPAN), bf16),
        fy=((2, D // 2, SPAN), bf16),
        gdt_all=((16, D), bf16),
        gdt=((n, 16, DS), bf16),
        rdt=((n + 1, 16, DS), bf16),
        bsum=((DS, 128), f32),
        bslot=((4, DS, 128), bf16),
        bfin=((2, DS, 128), bf16),
        ng=((1, D), f32),
        sv=((24, C), f32),
        pv=((24, C), f32),
        lslot=((n, 24, C), f32),
    )
    semaphores = dict(
        ag_s=(2, 13),
        ag_r=(2, 13),
        za_s=(5, 2, n - 1),
        za_r=(5, 2, n - 1),
        zr_s=(5, 2, n - 1),
        zr_r=(5, 2, n - 1),
        rs_s=(2, 10),
        rs_r=(2, 10),
        mate_s=(3,),
        mate_r=(3,),
        sum_s=(2, 8),
        sum_r=(2, 8),
        ls_s=(n,),
        ls_r=(n,),
        ps_s=(8,),
        ps_r=(8,),
        bc_s=(3,),
        bc_r=(3,),
        loc=(7,),
    )
    names = [*inputs, *outputs, *scratch, *semaphores, "free"]
    vmem = pl.BlockSpec(memory_space=pltpu.VMEM)
    hbm = pl.BlockSpec(memory_space=pl.ANY)
    smem = pl.BlockSpec(memory_space=pltpu.SMEM)
    where = {k: hbm for k in ("gcot", "wz", "wx", "wbc", "block_out", "grad_in")}
    where.update(lengths=smem, perm=smem)
    out = pl.pallas_call(
        functools.partial(kernel, names, n, C, H),
        out_shape=[jax.ShapeDtypeStruct(*s) for s in outputs.values()],
        in_specs=[where.get(k, vmem) for k in inputs],
        out_specs=[where.get(k, vmem) for k in outputs],
        scratch_shapes=[pltpu.VMEM(*s) for s in scratch.values()]
        + [pltpu.SemaphoreType.DMA(s) for s in semaphores.values()]
        + [pltpu.SemaphoreType.REGULAR((5,))],
        compiler_params=pltpu.CompilerParams(
            collective_id=0, has_side_effects=True, vmem_limit_bytes=(64 << 20) - (1 << 18)
        ),
    )(*inputs.values())

    results = dict(
        o_block=((rows, D), bf16),
        o_grad=((rows, D), bf16),
        o_ng=((D,), f32),
        o_z=((DS, C), f32),
        o_x=((DS, C), f32),
        o_dt=((DS, H), f32),
        o_bc=((DS, BC), f32),
        o_cx=((KERNEL, inner), f32),
        o_cxb=((inner,), f32),
        o_cbc=((KERNEL, BC), f32),
        o_cbcb=((BC,), f32),
        o_dtb=(dt_bias.shape, f32),
        o_alog=(a_log.shape, f32),
        o_skip=(skip_d.shape, f32),
        o_gate=((inner,), f32),
        o_wo=((C, DS), f32),
    )
    copied = ("o_block", "o_grad", "o_z", "o_x", "o_bc")
    place = lambda k: hbm if k in copied else vmem
    return pl.pallas_call(
        functools.partial(unpack, [*outputs, *results, "sem"], C, H),
        out_shape=[jax.ShapeDtypeStruct(*s) for s in results.values()],
        in_specs=[place(k) for k in outputs],
        out_specs=[place(k) for k in results],
        scratch_shapes=[pltpu.SemaphoreType.DMA((5,))],
    )(*out)


def solution(mesh):
    assert mesh.shape["row"] == 4 and mesh.shape["col"] == 2
    every = P(("dp", "row", "col"), None)
    weight = P("dp", ("row", "col"))
    out = P(("row", "col"), "dp")
    return jax.shard_map(
        functools.partial(shards, mesh.shape["dp"]),
        mesh=mesh,
        in_specs=(every, P(), P("dp"), P(), weight, weight, weight, P("dp", None))
        + (P(),) * 8
        + (out, every),
        out_specs=(every, every, P(), weight, weight, weight, P("dp", None)) + (P(),) * 8 + (out,),
        check_vma=False,
    )
```

```python
import functools
import types

import jax
import jax.numpy as jnp
from jax import lax
from jax.experimental import pallas as pl
from jax.experimental.pallas import tpu as pltpu
from jax.sharding import PartitionSpec as P

SPAN = 256
HALF = SPAN // 2
STATE = 128
BC = 2 * STATE
KERNEL = 4
EPS = 1e-5
f32, bf16 = jnp.float32, jnp.bfloat16
MESH = pl.DeviceIdType.MESH
LITTLE = ("w_dt", "gain", "conv_x", "conv_xb", "conv_bc", "conv_bcb", "dt_bias", "a_log", "skip", "gate")


def nt(a, b):
    return lax.dot_general(a, b, (((1,), (1,)), ((), ())), preferred_element_type=f32)


def nn(a, b):
    return lax.dot_general(a, b, (((1,), (0,)), ((), ())), preferred_element_type=f32)


def tn(a, b):
    return lax.dot_general(a, b, (((0,), (0,)), ((), ())), preferred_element_type=f32)


def aligned(start, size):
    return pl.ds(pl.multiple_of(start, size), size)


def softplus(v):
    return jnp.maximum(v, 0.0) + jnp.log1p(jnp.exp(-jnp.abs(v)))


def split3(v):
    a = v.astype(bf16)
    w = v - a.astype(f32)
    b = w.astype(bf16)
    return jnp.concatenate([a, b, (w - b.astype(f32)).astype(bf16)], axis=0)


def merge3(v):
    return v[0:8] + v[8:16] + v[16:24]


def tri_low():
    i = lax.broadcasted_iota(jnp.int32, (SPAN, SPAN), 0)
    j = lax.broadcasted_iota(jnp.int32, (SPAN, SPAN), 1)
    return (i >= j).astype(bf16)


def decay_terms(b, offs, da, flip=False):
    first = b * SPAN
    row = first + lax.broadcasted_iota(jnp.int32, (1, SPAN), 1)
    col = first + lax.broadcasted_iota(jnp.int32, (SPAN, 1), 0)

    def begin(pos):
        at = jnp.zeros_like(pos)
        for o in offs[1:]:
            at = jnp.where(pos >= o, o, at)
        return at

    beg_r, beg_c = begin(row), begin(col)
    l_row = merge3(nt(split3(da), tri_low()))
    l_col = l_row.T
    last = l_row[:, SPAN - 1 : SPAN]
    end_b = jnp.max(beg_r, axis=1, keepdims=True)
    e = jnp.where(beg_r < first, jnp.exp(l_row), 0.0)
    we = jnp.where(beg_r == end_b, jnp.exp(last - l_row), 0.0)
    kept = jnp.where(end_b < first, jnp.exp(last), 0.0)
    order = (col <= row) if flip else (row <= col)
    mask = jnp.where((beg_r == beg_c) & order, 1.0, 0.0)
    return l_row, l_col, e, we, kept, mask, row - beg_r


def wide(ref, k, rows):
    w = ref[k, rows, :]
    return jnp.concatenate([w, w], axis=1)


def fold(v):
    return v[:, 0:128] + v[:, 128:256]


def conv_forward(cur, tail, pref, rows, places):
    win = jnp.concatenate([tail, cur], axis=1)
    u = wide(pref, 3, rows) * cur + wide(pref, 4, rows)
    for s in (1, 2, 3):
        back = jnp.where(places >= s, pltpu.roll(win, s, 1)[:, 128:], 0.0)
        u = u + wide(pref, 3 - s, rows) * back
    return u


def conv_backward(R, raw, du, pref, acc, head, rows, base, tok, m):
    out = wide(pref, 3, rows) * du
    acc[4, rows, :] += fold(du)
    acc[3, rows, :] += fold(du * raw)
    for s in (1, 2, 3):
        w = du * m[s]
        win = jnp.concatenate([w, head[s - 1, rows, :]], axis=1)
        sh = pltpu.roll(win, SPAN + 128 - s, 1)[:, 0:SPAN]
        head[s - 1, rows, :] = w[:, 0:128]
        out = out + wide(pref, 3 - s, rows) * sh
        acc[3 - s, rows, :] += fold(sh * raw)
    R.dcat[base + rows.start : base + rows.stop, tok] = out.astype(bf16)


def scan_block(b, R, offs, C, H):
    p = C // H
    tok = aligned(b * SPAN, SPAN)
    R.pr[...] = nt(R.wcat[C:, :], R.hn[tok, :])
    R.xr[:, tok] = R.pr[0:C, :].astype(bf16)
    R.bcr[:, tok] = R.pr[C : C + BC, :].astype(bf16)
    dr = R.pr[C + BC : C + BC + 8, :] + R.ph[:, 0:1]
    R.dr[:, tok] = dr
    dt = softplus(dr)
    l_row, l_col, e, we, kept, mask, places = decay_terms(b, offs, dt * R.ph[:, 1:2], True)
    bcr = R.pr[C : C + BC, :]
    u = conv_forward(bcr, R.tail_bc[...], R.pbc, slice(0, BC), places).astype(bf16)
    R.tail_bc[...] = bcr[:, 128:]
    R.ubc[:, tok] = u
    u = u.astype(f32)
    bc = (u * jax.nn.sigmoid(u)).astype(bf16)
    bt, ct = bc[0:STATE, :], bc[STATE:BC, :]
    R.gm[...] = tn(bt, ct) * mask
    for h in range(H):
        rows = slice(h * p, (h + 1) * p)
        hh = slice(h, h + 1)
        xr = R.pr[rows, :]
        u = conv_forward(xr, R.tail_x[rows, :], R.px, rows, places).astype(bf16)
        R.tail_x[rows, :] = xr[:, 128:]
        R.ux[rows, tok] = u
        u = u.astype(f32)
        xd = u * jax.nn.sigmoid(u) * dt[hh, :]
        d = jnp.exp(jnp.minimum(l_row[hh, :] - l_col[:, hh], 0.0))
        mix = (d * R.gm[...]).astype(bf16)
        st = R.state[rows, :]
        stb = st.astype(bf16)
        R.states[b, rows, :] = stb
        R.y[rows, tok] = nn(xd.astype(bf16), mix) + nn(stb, ct) * e[hh, :]
        R.state[rows, :] = kept[hh, :] * st + nt((xd * we[hh, :]).astype(bf16), bt)


def gate_block(b, R, C, H):
    p = C // H
    tok = aligned(b * SPAN, SPAN)
    R.z[:, tok] = nt(R.wcat[0:C, :], R.hn[tok, :]).astype(bf16)
    sq = jnp.zeros((1, SPAN), f32)
    for h in range(H):
        rows = slice(h * p, (h + 1) * p)
        u = R.ux[rows, tok].astype(f32)
        zz = R.z[rows, tok].astype(f32)
        yf = R.y[rows, tok] + wide(R.px, 6, rows) * (u * jax.nn.sigmoid(u))
        gy = yf * (zz * jax.nn.sigmoid(zz))
        sq = sq + jnp.sum(gy * gy, axis=0, keepdims=True)
        R.gg[rows, tok] = (gy * wide(R.px, 5, rows)).astype(bf16)
    R.sums[0, pl.ds(b, 1), :] = sq


def gate_back_block(b, R, C, H, inner):
    p = C // H
    tok = aligned(b * SPAN, SPAN)
    r = lax.rsqrt(R.tot[0, pl.ds(b, 1), :] / inner + EPS)
    rs = r * r * R.tot[1, pl.ds(b, 1), :] / inner
    for h in range(H):
        rows = slice(h * p, (h + 1) * p)
        u = R.ux[rows, tok].astype(f32)
        x = u * jax.nn.sigmoid(u)
        zz = R.z[rows, tok].astype(f32)
        sz = jax.nn.sigmoid(zz)
        gate = zz * sz
        yf = R.y[rows, tok] + wide(R.px, 6, rows) * x
        gy = yf * gate
        dyn = R.dyn[rows, tok].astype(f32)
        R.accx[5, rows, :] += fold(dyn * (gy * r))
        dgy = (r * wide(R.px, 5, rows)) * dyn - gy * rs
        R.dcat[rows, tok] = (dgy * yf * (sz + gate * (1.0 - sz))).astype(bf16)
        dy = dgy * gate
        R.accx[6, rows, :] += fold(dy * x)
        R.dyn[rows, tok] = dy.astype(bf16)


def bwd_block(b, R, offs, C, H):
    p = C // H
    tok = aligned(b * SPAN, SPAN)
    v = R.dr[:, tok]
    dt = softplus(v)
    rate = R.ph[:, 1:2]
    l_row, l_col, e, we, kept, mask, places = decay_terms(b, offs, dt * rate)
    ubc = R.ubc[:, tok].astype(f32)
    sg = jax.nn.sigmoid(ubc)
    bc = (ubc * sg).astype(bf16)
    bt, ct = bc[0:STATE, :], bc[STATE:BC, :]
    R.gm[...] = tn(ct, bt) * mask
    m = [None] + [jnp.where(places >= s, 1.0, 0.0) for s in (1, 2, 3)]
    decays, directs, ends = [], [], []
    for h in range(H):
        rows = slice(h * p, (h + 1) * p)
        hh = slice(h, h + 1)
        u = R.ux[rows, tok].astype(f32)
        sx = jax.nn.sigmoid(u)
        x = u * sx
        y = R.y[rows, tok]
        dyb = R.dyn[rows, tok]
        dy = dyb.astype(f32)
        xd = x * dt[hh, :]
        xdb = xd.astype(bf16)
        d = jnp.exp(jnp.minimum(l_col[:, hh] - l_row[hh, :], 0.0))
        mix = (d * R.gm[...]).astype(bf16)
        vin = nn(dyb, mix)
        dm = tn(dyb, xdb) * d
        if h == 0:
            R.dg[...] = dm
        else:
            R.dg[...] += dm
        stb = R.states[b, rows, :]
        lam = R.state[rows, :]
        lamb = lam.astype(bf16)
        lb = nn(lamb, bt) * we[hh, :]
        vt = vin + lb
        xlow = xdb.astype(f32)
        decays.append(jnp.sum(dy * y - xlow * vt, axis=0, keepdims=True))
        directs.append(jnp.sum(x * vt, axis=0, keepdims=True))
        through = jnp.sum(lam * stb.astype(f32), axis=0, keepdims=True) * kept[hh, :]
        ends.append(
            jnp.sum(xlow * lb, axis=0, keepdims=True)
            + jnp.concatenate([through, jnp.zeros((1, SPAN - STATE), f32)], axis=1)
        )
        edy = (dy * e[hh, :]).astype(bf16)
        R.edy[rows, :] = edy
        R.wxd[rows, :] = (xd * we[hh, :]).astype(bf16)
        R.lamb[rows, :] = lamb
        R.state[rows, :] = kept[hh, :] * lam + nt(edy, ct)
        dx = dt[hh, :] * vt + wide(R.px, 6, rows) * dy
        du = dx * (sx + x * (1.0 - sx))
        conv_backward(R, R.xr[rows, tok].astype(f32), du, R.px, R.accx, R.head_x, rows, C, tok, m)
    dgm = (R.dg[...] * mask).astype(bf16)
    dct = nt(bt, dgm) + tn(R.states[b], R.edy[...])
    dbt = nn(ct, dgm) + tn(R.lamb[...], R.wxd[...])
    du = jnp.concatenate([dbt, dct], axis=0) * (sg + ubc * sg * (1.0 - sg))
    conv_backward(
        R, R.bcr[:, tok].astype(f32), du, R.pbc, R.accbc, R.head_bc, slice(0, BC), 2 * C, tok, m
    )
    pad = [jnp.zeros((8 - H, SPAN), f32)]
    end = jnp.sum(jnp.concatenate(ends + pad, axis=0), axis=1, keepdims=True)
    g = merge3(nn(split3(jnp.concatenate(decays + pad, axis=0)), tri_low())) + end
    ddr = (g * rate + jnp.concatenate(directs + pad, axis=0)) * jax.nn.sigmoid(v)
    R.acch[0] += ddr
    R.acch[1] += g * dt * rate
    R.dcat[2 * C + BC : 2 * C + BC + 16, tok] = jnp.concatenate(
        [ddr, jnp.zeros((8, SPAN), f32)], axis=0
    ).astype(bf16)


def remote(src, dst, send, recv, device):
    return pltpu.make_async_remote_copy(
        src_ref=src, dst_ref=dst, send_sem=send, recv_sem=recv, device_id=device, device_id_type=MESH
    )


class Place:
    def __init__(self, n):
        self.n = n
        self.dp, self.row, self.col = (lax.axis_index(a) for a in ("dp", "row", "col"))
        self.x, self.c, self.y = self.row // 2, self.row % 2, self.col
        self.q = self.index(self.x, self.c, self.y)
        self.mate = (self.dp, self.x * 2 + 1 - self.c, self.y)
        self.xn = (self.dp, (1 - self.x) * 2 + self.c, self.y)
        self.yn = (self.dp, self.row, 1 - self.y)
        self.diag = (self.dp, (1 - self.x) * 2 + self.c, 1 - self.y)

    def index(self, x, c, y):
        return (x * 2 + c) * 2 + y

    def plane(self, d):
        k = (self.q + d) % 8
        return k, (self.dp, k // 2, k % 2)

    def line(self, d):
        k = (self.dp + d) % self.n
        return k, (k, self.row, self.col)

    def right(self):
        return (self.dp + 1, self.row, self.col)

    def left(self):
        return (self.dp - 1, self.row, self.col)


class PlaneGather:
    def __init__(self, me, buf, send, recv):
        self.me, self.buf, self.send, self.recv = me, buf, send, recv
        x, c, y = me.x, me.c, me.y
        own = lambda cc: (
            me.index(x, cc, y),
            me.index(1 - x, cc, y),
            me.index(x, cc, 1 - y),
            me.index(1 - x, cc, 1 - y),
        )
        self.q, self.qx, self.qy, self.qd = own(c)
        self.mq, self.mx, self.my, self.md = own(1 - c)

    def at(self, k, half):
        if half is None:
            return self.buf.at[aligned(k * SPAN, SPAN), :]
        return self.buf.at[aligned(k * SPAN + half * HALF, HALF), :]

    def copy(self, i, k, half, device):
        region = self.at(k, half)
        return remote(region, region, self.send.at[i], self.recv.at[i], device)

    def wait(self, i, k, half):
        self.copy(i, k, half, self.me.mate).wait_recv()

    def start(self):
        me = self.me
        self.copy(0, self.q, 0, me.xn).start()
        self.copy(3, self.q, 1, me.yn).start()
        self.copy(1, self.q, 1, me.xn).start()
        self.copy(2, self.q, 0, me.yn).start()
        self.copy(6, self.q, None, me.mate).start()

    def step1(self):
        me = self.me
        self.wait(0, self.qx, 0)
        self.copy(4, self.qx, 0, me.yn).start()
        self.copy(7, self.qx, 0, me.mate).start()
        self.wait(3, self.qy, 1)
        self.copy(5, self.qy, 1, me.xn).start()
        self.copy(10, self.qy, 1, me.mate).start()

    def step2(self):
        me = self.me
        self.wait(1, self.qx, 1)
        self.copy(8, self.qx, 1, me.mate).start()
        self.wait(2, self.qy, 0)
        self.copy(9, self.qy, 0, me.mate).start()

    def step3(self):
        me = self.me
        self.wait(4, self.qd, 0)
        self.copy(11, self.qd, 0, me.mate).start()
        self.wait(5, self.qd, 1)
        self.copy(12, self.qd, 1, me.mate).start()

    def step4(self):
        self.wait(6, self.mq, None)
        self.wait(7, self.mx, 0)
        self.wait(8, self.mx, 1)
        self.wait(9, self.my, 0)
        self.wait(10, self.my, 1)
        self.wait(11, self.md, 0)
        self.wait(12, self.md, 1)
        for i in range(13):
            self.copy(i, self.q, None if i == 6 else 0, self.me.mate).wait_send()


def both(*conds):
    out = conds[0]
    for c in conds[1:]:
        out = jnp.logical_and(out, c)
    return out


class LineGather:
    def __init__(self, me, at, send, recv):
        self.me, self.at, self.send, self.recv = me, at, send, recv

    def copy(self, way, s, k):
        device = self.me.right() if way == 0 else self.me.left()
        return remote(self.at(k), self.at(k), self.send.at[way, s], self.recv.at[way, s], device)

    def start(self):
        me = self.me

        @pl.when(me.dp < me.n - 1)
        def _():
            self.copy(0, 0, me.dp).start()

        @pl.when(me.dp > 0)
        def _():
            self.copy(1, 0, me.dp).start()

    def step(self, s):
        me = self.me
        k = me.dp - 1 - s
        j = me.dp + 1 + s

        @pl.when(k >= 0)
        def _():
            self.copy(0, s, k).wait_recv()

        @pl.when(j <= me.n - 1)
        def _():
            self.copy(1, s, j).wait_recv()

        @pl.when(both(me.dp < me.n - 1, me.dp - s >= 0))
        def _():
            self.copy(0, s, me.dp).wait_send()

        @pl.when(both(me.dp > 0, me.dp + s <= me.n - 1))
        def _():
            self.copy(1, s, me.dp).wait_send()

        @pl.when(both(k >= 0, me.dp < me.n - 1, s < me.n - 2))
        def _():
            self.copy(0, s + 1, k).start()

        @pl.when(both(j <= me.n - 1, me.dp > 0, s < me.n - 2))
        def _():
            self.copy(1, s + 1, j).start()


class LineScatter:
    def __init__(self, me, src, slot, send, recv):
        self.me, self.src, self.slot, self.send, self.recv = me, src, slot, send, recv

    def copy(self, way, s, what, to):
        (a, i), (b, j) = what, to
        device = self.me.right() if way == 0 else self.me.left()
        return remote(a.at[i], b.at[j], self.send.at[way, s], self.recv.at[way, s], device)

    def got(self, way, s, slot):
        self.copy(way, s, slot, slot).wait_recv()

    def add(self, k):
        (a, i), (b, j) = self.slot(k), self.src(k)
        a[i] = (a[i].astype(f32) + b[j].astype(f32)).astype(bf16)

    def moves(self, t):
        me, n = self.me, self.me.n
        s, v = t - me.dp, t - (n - 1 - me.dp)
        return both(s >= 0, n - 1 - s > me.dp), s, n - 1 - s, both(v >= 0, v < me.dp), v, v

    def slot_step(self, t):
        me, n = self.me, self.me.n
        to_right, s, k, to_left, v, j = self.moves(t)

        @pl.when(both(to_right, me.dp > 0))
        def _():
            self.got(0, s, self.slot(k))
            self.add(k)
            self.copy(0, s, self.slot(k), self.slot(k)).start()

        @pl.when(both(to_right, me.dp == 0))
        def _():
            self.copy(0, s, self.src(k), self.slot(k)).start()

        to = self.slot(jnp.where(j == me.dp - 1, n, j))

        @pl.when(both(to_left, me.dp < n - 1))
        def _():
            self.got(1, v, self.slot(j))
            self.add(j)
            self.copy(1, v, self.slot(j), to).start()

        @pl.when(both(to_left, me.dp == n - 1))
        def _():
            self.copy(1, v, self.src(j), to).start()

    def total(self, put):
        me, n = self.me, self.me.n
        a, i = self.src(me.dp)
        put(a[i].astype(f32), True)

        @pl.when(me.dp > 0)
        def _():
            b, j = self.slot(me.dp)
            self.got(0, n - 1 - me.dp, (b, j))
            put(b[j].astype(f32), False)

        @pl.when(me.dp < n - 1)
        def _():
            b, j = self.slot(n)
            self.got(1, me.dp, (b, j))
            put(b[j].astype(f32), False)

    def finish(self, t):
        to_right, s, k, to_left, v, j = self.moves(t)

        @pl.when(to_right)
        def _():
            self.copy(0, s, self.src(0), self.slot(0)).wait_send()

        @pl.when(to_left)
        def _():
            self.copy(1, v, self.src(0), self.slot(0)).wait_send()


class PlaneScatter:
    def __init__(self, me, R, send, recv, part, credit):
        self.me, self.R, self.send, self.recv, self.part, self.credit = me, R, send, recv, part, credit
        x, y = me.x, me.y
        self.jo, self.jx, self.jy, self.jd = x * 2 + y, (1 - x) * 2 + y, x * 2 + 1 - y, (1 - x) * 2 + 1 - y

    def copy(self, i, src, dst, device):
        return remote(src, dst, self.send.at[i], self.recv.at[i], device)

    def block(self, t):
        me = self.me
        dx, dy = 1 - t // 2, 1 - t % 2
        return me.x + dx * (1 - 2 * me.x), me.y + dy * (1 - 2 * me.y)

    def for_mate(self, t):
        me, R = self.me, self.R
        xx, yy = self.block(t)
        k = me.index(xx, 1 - me.c, yy)
        slot = R.sb.at[t % 2]

        @pl.when(t >= 2)
        def _():
            self.copy(t - 2, slot, slot, me.mate).wait_send()

        R.sb[t % 2, 0] = self.part(k, 0).astype(bf16)
        R.sb[t % 2, 1] = self.part(k, 1).astype(bf16)
        self.copy(t, slot, R.rb.at[xx * 2 + yy], me.mate).start()

    def for_this(self, t):
        me, R = self.me, self.R
        xx, yy = self.block(t)
        j = xx * 2 + yy
        k = me.index(xx, me.c, yy)
        self.copy(t, R.rb.at[j], R.rb.at[j], me.mate).wait_recv()
        R.rb[j, 0] = (self.part(k, 0) + R.rb[j, 0].astype(f32)).astype(bf16)
        R.rb[j, 1] = (self.part(k, 1) + R.rb[j, 1].astype(f32)).astype(bf16)

        @pl.when(t == 0)
        def _():
            self.copy(4, R.rb.at[self.jd, 0], R.da, me.xn).start()
            self.copy(5, R.rb.at[self.jd, 1], R.db, me.yn).start()

        @pl.when(t == 1)
        def _():
            self.copy(6, R.rb.at[self.jx, 0], R.fx.at[0], me.xn).start()

        @pl.when(t == 2)
        def _():
            self.copy(9, R.rb.at[self.jy, 1], R.fy.at[1], me.yn).start()

    def blocks(self, beside):
        if self.credit:
            for i in (1, 2):
                pl.semaphore_wait(self.R.free.at[i], 1)

        @pl.loop(0, 5)
        def _(t):
            @pl.when(t < 4)
            def _():
                self.for_mate(t)

            @pl.when(t > 0)
            def _():
                self.for_this(t - 1)

            beside(t)

    def relay(self):
        me, R = self.me, self.R
        self.copy(4, R.da, R.da, me.xn).wait_recv()
        R.rb[self.jy, 0] = (R.rb[self.jy, 0].astype(f32) + R.da[...].astype(f32)).astype(bf16)
        self.copy(8, R.rb.at[self.jy, 0], R.fy.at[0], me.yn).start()
        self.copy(5, R.db, R.db, me.yn).wait_recv()
        R.rb[self.jx, 1] = (R.rb[self.jx, 1].astype(f32) + R.db[...].astype(f32)).astype(bf16)
        self.copy(7, R.rb.at[self.jx, 1], R.fx.at[1], me.xn).start()

    def total(self, put):
        me, R = self.me, self.R
        for half in (0, 1):
            self.copy(6 + half, R.fx.at[half], R.fx.at[half], me.xn).wait_recv()
            self.copy(8 + half, R.fy.at[half], R.fy.at[half], me.yn).wait_recv()
            steps = R.da.shape[0] // 128

            @pl.loop(0, steps)
            def _(i):
                rows = aligned(i * 128, 128)
                v = R.rb[self.jo, half, rows, :].astype(f32)
                put(half * steps + i, v + R.fx[half, rows, :].astype(f32) + R.fy[half, rows, :].astype(f32))

    def finish(self, release):
        me, R = self.me, self.R
        for i in (2, 3):
            self.copy(i, R.sb.at[0], R.sb.at[0], me.mate).wait_send()
        for i in range(4, 10):
            self.copy(i, R.da, R.db, me.mate).wait_send()
        if release:
            for i, device in enumerate((me.mate, me.xn, me.yn)):
                pl.semaphore_signal(R.free.at[i], 1, device_id=device, device_id_type=MESH)


def stepped(n, *fns):
    if n <= 4:
        return [lambda s=s: [f(s) for f in fns] for s in range(n - 1)]

    def every():
        @pl.loop(0, n - 1)
        def _(s):
            for f in fns:
                f(s)

    return [every] + [lambda: None] * 2


def kernel(names, n, C, H, *refs):
    R = types.SimpleNamespace(**dict(zip(names, refs)))
    me = Place(n)
    T, D = R.hn.shape
    inner = R.gate.shape[0]
    heads = R.skip.shape[0]
    nb = T // SPAN
    DS = D // n
    dp = me.dp
    rows = 2 * C + BC + 16
    dt_rows = slice(2 * C + BC, rows)
    share = lambda k: pl.ds(pl.multiple_of(k * DS, 16), DS)
    dhalf = lambda h: slice(h * (D // 2), (h + 1) * (D // 2))
    half = aligned(2 * C + me.c * 128, 128)
    other = aligned(2 * C + (1 - me.c) * 128, 128)

    def over(length):
        def run(f):
            pl.loop(0, length)(f)

        return run

    def beside(i, polls):
        for k, fns in polls.items():

            @pl.when(i == k)
            def _():
                for f in fns:
                    f()

    stage = lambda a, z: R.y.at[0:DS, a:z]
    arriving = [
        pltpu.make_async_copy(src, dst, R.loc.at[i])
        for i, (src, dst) in enumerate(
            (
                (R.wx, stage(C, 2 * C)),
                (R.wbc, stage(2 * C, 2 * C + BC)),
                (R.wz, stage(0, C)),
                (R.gcot, R.cot.at[aligned(me.q * SPAN, SPAN), :]),
                (R.wo, R.wo_own),
                (R.hidden_in, R.hid),
            )
        )
    ]
    little = [
        pltpu.make_async_copy(getattr(R, "in_" + k), getattr(R, k), R.loc.at[12 + i])
        for i, k in enumerate(LITTLE)
    ]
    for copy in arriving + little:
        copy.start()
    barrier = pltpu.get_barrier_semaphore()
    for d in range(1, 8):
        pl.semaphore_signal(barrier, 1, device_id=me.plane(d)[1], device_id_type=MESH)
    for d in range(1, n):
        pl.semaphore_signal(barrier, 1, device_id=me.line(d)[1], device_id_type=MESH)
    for copy in little:
        copy.wait()
    R.gains[...] = R.gain[...].reshape(1, D)
    arriving[5].wait()

    @over(SPAN // 32)
    def _(i):
        u = R.hid[aligned(i * 32, 32), :].astype(f32)
        qn = lax.rsqrt(jnp.mean(u * u, axis=1, keepdims=True) + EPS)
        R.hn[aligned(me.q * SPAN + i * 32, 32), :] = (u * qn * R.gains[...]).astype(bf16)

    for copy in arriving[:2]:
        copy.wait()
    R.wd[share(dp), C : 2 * C] = R.y[0:DS, C : 2 * C].astype(bf16)
    R.wd[share(dp), half] = R.y[0:DS, half].astype(bf16)
    R.wdt[dp] = jnp.concatenate([R.w_dt[...], jnp.zeros((16 - H, DS), f32)], axis=0).astype(bf16)
    pl.semaphore_wait(barrier, 7 + n - 1)

    tokens = PlaneGather(me, R.hn, R.ag_s.at[0], R.ag_r.at[0])
    cots = PlaneGather(me, R.cot, R.ag_s.at[1], R.ag_r.at[1])
    places = (
        lambda k: R.wd.at[share(k), C : 2 * C],
        lambda k: R.wd.at[share(k), half],
        lambda k: R.wdt.at[k],
        lambda k: R.wd.at[share(k), 0:C],
        lambda k: R.wot.at[share(k), :],
    )
    gathers = [LineGather(me, at, R.za_s.at[i], R.za_r.at[i]) for i, at in enumerate(places)]
    z_gather, wo_gather = gathers[3:]
    tokens.start()
    for g in gathers[:3]:
        g.start()

    for copy in arriving[2:5]:
        copy.wait()
    R.wd[share(dp), 0:C] = R.y[0:DS, 0:C].astype(bf16)
    R.wot[share(dp), :] = R.wo_own[...].T.astype(bf16)
    own = aligned(me.q * C, C)
    taps = [R.conv_x[:, own]]
    for v in (R.conv_xb, R.gate):
        R.row[...] = v[...].reshape(1, inner)
        taps.append(R.row[:, own])
    taps = jnp.concatenate(taps + [jnp.zeros((2, C), f32)], axis=0).T
    chan = lax.broadcasted_iota(jnp.int32, (C, heads), 0) // (C // H) + me.q * H
    pick = chan == lax.broadcasted_iota(jnp.int32, (C, heads), 1)
    skips = jnp.sum(jnp.where(pick, R.skip[...].reshape(1, heads), 0.0), axis=1, keepdims=True)
    for k in range(6):
        R.px[k] = jnp.broadcast_to(taps[:, k : k + 1], (C, 128))
    R.px[6] = jnp.broadcast_to(skips, (C, 128))
    taps = jnp.concatenate([R.conv_bc[...], R.conv_bcb[...].reshape(1, BC), jnp.zeros((3, BC), f32)], axis=0).T
    for k in range(5):
        R.pbc[k] = jnp.broadcast_to(taps[:, k : k + 1], (BC, 128))
    head = lax.broadcasted_iota(jnp.int32, (8, heads), 0)
    pick = (head + me.q * H == lax.broadcasted_iota(jnp.int32, (8, heads), 1)) & (head < H)
    R.ph[:, 0:1] = jnp.sum(jnp.where(pick, R.dt_bias[...].reshape(1, heads), 0.0), axis=1, keepdims=True)
    R.ph[:, 1:2] = jnp.sum(
        jnp.where(pick, -jnp.exp(R.a_log[...].reshape(1, heads)), 0.0), axis=1, keepdims=True
    )
    for a in (R.tail_bc, R.tail_x, R.state, R.head_x, R.head_bc, R.accx, R.accbc, R.acch, R.sv):
        a[...] = jnp.zeros_like(a)
    offs = [0]
    for k in range(R.perm.shape[0] - 1):
        offs.append(offs[-1] + R.lengths[R.perm[k]])

    def line(*fns):
        if n <= 4:
            return [lambda s=s: [f(s) for f in fns] for s in range(n - 1)] + [lambda: None] * (4 - n)

        def every():
            @over(n - 1)
            def _(s):
                for f in fns:
                    f(s)

        return [every] + [lambda: None] * 2

    def prepare(a, z):
        for k in range(a, z, 128):
            R.wcat[k : k + 128, :] = R.wd[:, k : k + 128].T

    steps = line(*[g.step for g in gathers[:3]])
    tokens.step1()
    steps[0]()
    tokens.step2()
    steps[1]()
    tokens.step3()
    cots.start()
    steps[2]()
    z_gather.start()
    bc_swap = remote(R.wd.at[:, half], R.wd.at[:, half], R.mate_s.at[0], R.mate_r.at[0], me.mate)
    bc_swap.start()
    prepare(C, 2 * C)
    for k in range(n):
        R.wcat[dt_rows, k * DS : (k + 1) * DS] = R.wdt[k]
    pad = jnp.zeros((112, D), bf16)
    R.wd[:, 2 * C + BC : 2 * C + BC + 128] = jnp.concatenate([R.wcat[dt_rows, :], pad], axis=0).T
    remote(R.wd.at[:, other], R.wd.at[:, other], R.mate_s.at[0], R.mate_r.at[0], me.mate).wait_recv()
    bc_swap.wait_send()
    prepare(2 * C, 2 * C + BC)
    tokens.step4()

    steps = line(z_gather.step)
    polls = {1: [steps[0]], 2: [cots.step1], 4: [steps[1]], 5: [cots.step2], 6: [steps[2], wo_gather.start]}

    @over(nb)
    def _(b):
        scan_block(b, R, offs, C, H)
        beside(b, polls)

    prepare(0, C)

    @over(nb)
    def _(b):
        gate_block(b, R, C, H)

    def share_sums(i):
        for d in range(1, 8):
            k, device = me.plane(d)
            remote(R.sums.at[i], R.sslot.at[i, me.q], R.sum_s.at[i, k], R.sum_r.at[i, me.q], device).start()
        R.sslot[i, me.q] = R.sums[i]

    def total_sums(i):
        for d in range(1, 8):
            k, device = me.plane(d)
            remote(R.sums.at[i], R.sslot.at[i, k], R.sum_s.at[i, k], R.sum_r.at[i, k], device).wait()
        total = R.sslot[i, 0]
        for k in range(1, 8):
            total = total + R.sslot[i, k]
        R.tot[i] = total

    share_sums(0)
    steps = line(wo_gather.step)
    steps[0]()
    cots.step3()
    cots.step4()
    total_sums(0)

    @over(nb)
    def _(b):
        tok = aligned(b * SPAN, SPAN)
        r = lax.rsqrt(R.tot[0, pl.ds(b, 1), :] / inner + EPS)
        R.gg[:, tok] = (R.gg[:, tok].astype(f32) * r).astype(bf16)

    @over(D // 256)
    def _(i):
        some = aligned(i * 256, 256)
        R.won[some, :] = nn(R.gg[...], R.cot[:, some]).astype(bf16).T

    def scatter(i, src, lanes):
        slot = lambda k: (R.cot, (share(k), slice(*lanes)))
        return LineScatter(me, src, slot, R.zr_s.at[i], R.zr_r.at[i])

    wo_slot = lambda k: (
        R.dcat,
        (pl.ds(pl.multiple_of(C + k // 5 * DS, 16), DS), aligned(k % 5 * C, C)),
    )
    wo_sum = LineScatter(me, lambda k: (R.won, (share(k), slice(0, C))), wo_slot, R.zr_s.at[0], R.zr_r.at[0])
    x_sum = scatter(1, lambda k: (R.won, (share(k), slice(0, C))), (C, 2 * C))
    z_sum = scatter(2, lambda k: (R.wot, (share(k), slice(0, C))), (0, C))
    dt_sum = LineScatter(
        me, lambda k: (R.gdt, (k,)), lambda k: (R.rdt, (k,)), R.zr_s.at[4], R.zr_r.at[4]
    )
    wo_steps = line(wo_sum.slot_step)
    steps[1]()
    wo_steps[0]()
    steps[2]()
    for k in range(0, D, 256):
        R.wout[:, k : k + 256] = R.wot[k : k + 256, :].T

    @over(nb)
    def _(b):
        tok = aligned(b * SPAN, SPAN)
        dyn = nt(R.wout[...], R.cot[tok, :])
        R.dyn[:, tok] = dyn.astype(bf16)
        R.sums[1, pl.ds(b, 1), :] = jnp.sum(dyn * R.gg[:, tok].astype(f32), axis=0, keepdims=True)

    share_sums(1)

    @pl.when(dp < n - 1)
    def _():
        pl.semaphore_signal(R.free.at[3], 1, device_id=me.right(), device_id_type=MESH)

    @pl.when(dp > 0)
    def _():
        pl.semaphore_signal(R.free.at[4], 1, device_id=me.left(), device_id_type=MESH)

    mixed = PlaneScatter(
        me,
        R,
        R.rs_s.at[0],
        R.rs_r.at[0],
        lambda k, h: nn(R.wot[dhalf(h), :], R.gg[:, aligned(k * SPAN, SPAN)]),
        False,
    )
    wo_steps[1]()
    mixed.blocks(lambda t: beside(t, {3: [wo_steps[2]]}))
    total_sums(1)

    @over(nb)
    def _(b):
        gate_back_block(b, R, C, H, inner)

    def weight_grad(a, z, dst, at):
        @over(D // 256)
        def _(i):
            some = aligned(i * 256, 256)
            g = nn(R.dcat[a:z, :], R.hn[:, some])
            R.ng[:, some] += jnp.sum(g * R.wcat[a:z, some].astype(f32), axis=0, keepdims=True)
            g = g.astype(bf16)
            w = z - a
            if z == rows:
                w -= 16
                R.gdt_all[:, some] = g[w:]
            dst[some, at : at + w] = g[0:w].T

    R.ng[...] = jnp.zeros_like(R.ng)
    weight_grad(0, C, R.wot, 0)

    @pl.when(dp > 0)
    def _():
        pl.semaphore_wait(R.free.at[3], 1)

    @pl.when(dp < n - 1)
    def _():
        pl.semaphore_wait(R.free.at[4], 1)

    z_steps = line(z_sum.slot_step)
    z_steps[0]()

    def put(ref):
        def f(v, new):
            if new:
                ref[...] = v
            else:
                ref[...] += v

        return f

    out_copy = pltpu.make_async_copy(R.wout.at[0:SPAN, :], R.out_block, R.loc.at[6])

    leaving = [
        pltpu.make_async_copy(a, b, R.loc.at[i])
        for i, (a, b) in enumerate(
            (
                (R.gwo, R.out_wo),
                (R.gz, R.out_z),
                (R.gbc, R.out_bc),
                (R.gx, R.out_x),
                (R.small, R.out_small),
                (R.gdt_out, R.out_dt),
            )
        )
    ]

    def finish_mixed():
        def put(k, v):
            cols = aligned(k * 128, 128)
            R.wout[0:SPAN, cols] = (R.hid[:, cols].astype(f32) + v.T).astype(bf16)

        mixed.total(put)
        out_copy.start()
        mixed.finish(True)

    wo_sum.total(put(R.gwo))
    leaving[0].start()
    for s in line(wo_sum.finish):
        s()
    R.state[...] = jnp.zeros_like(R.state)
    polls = {0: [mixed.relay], 2: [z_steps[1]], 5: [z_steps[2]]}

    @over(nb)
    def _(i):
        bwd_block(nb - 1 - i, R, offs, C, H)
        beside(i, polls)

    weight_grad(2 * C, rows, R.cot, 2 * C + 128)
    finish_mixed()
    for k in range(n):
        R.gdt[k] = R.gdt_all[:, k * DS : (k + 1) * DS]
    bx = R.cot.at[0:D, 2 * C + 384 : 2 * C + 512]
    bc_own = aligned(2 * C + 128 + me.c * 128, 128)
    bc_other = aligned(2 * C + 256 - me.c * 128, 128)
    bc_pair = remote(R.cot.at[0:D, bc_other], bx, R.mate_s.at[1], R.mate_r.at[1], me.mate)
    bc_sum = scatter(3, lambda k: (R.cot, (share(k), bc_own)), (2 * C, 2 * C + 128))
    bc_steps = line(bc_sum.slot_step, dt_sum.slot_step)
    x_steps = line(x_sum.slot_step)
    pl.semaphore_wait(R.free.at[0], 1)
    bc_pair.start()
    weight_grad(C, 2 * C, R.won, 0)
    bc_pair.wait()
    R.cot[0:D, bc_own] = (R.cot[0:D, bc_own].astype(f32) + bx[...].astype(f32)).astype(bf16)
    bc_steps[0]()
    x_steps[0]()

    dhn = PlaneScatter(
        me,
        R,
        R.rs_s.at[1],
        R.rs_r.at[1],
        lambda k, h: nn(R.wd[dhalf(h), 0:rows], R.dcat[:, aligned(k * SPAN, SPAN)]),
        True,
    )
    dhn.blocks(lambda t: beside(t, {2: [bc_steps[1]], 4: [bc_steps[2], x_steps[1]]}))

    ax = [jnp.sum(R.accx[k], axis=1, keepdims=True) for k in range(7)]
    ab = [jnp.sum(R.accbc[k], axis=1, keepdims=True) for k in range(5)]
    ah = [jnp.sum(R.acch[k], axis=1, keepdims=True) for k in range(2)]
    p = C // H
    ah += [jnp.sum(ax[6][h * p : (h + 1) * p], axis=0, keepdims=True) for h in range(H)]
    ah = jnp.concatenate(ah + [jnp.zeros((8 - H, 1), f32)], axis=0)
    R.sv[0:8, :] = jnp.concatenate(ax[:6] + [jnp.zeros((C, 2), f32)], axis=1).T
    R.sv[6:7, 0:128] = jnp.concatenate(
        [jnp.broadcast_to(ah, (24, 128)), jnp.zeros((104, 128), f32)], axis=0
    ).T[0:1, :]
    R.sv[8:16, 0:BC] = jnp.concatenate(ab + [jnp.zeros((BC, 3), f32)], axis=1).T
    ng = R.ng[...] / R.gains[...]
    for k in range(D // C):
        R.sv[16 + k : 17 + k, :] = ng[:, k * C : (k + 1) * C]
    for d in range(1, n):
        k, device = me.line(d)
        remote(R.sv, R.lslot.at[dp], R.ls_s.at[k], R.ls_r.at[dp], device).start()
    R.lslot[dp] = R.sv[...]
    bc_sum.total(put(R.bsum))
    j = me.x * 2 + me.y
    R.bslot[j] = R.bsum[...].astype(bf16)
    crossing = []
    for i, (device, k) in enumerate(
        ((me.xn, (1 - me.x) * 2 + me.y), (me.yn, me.x * 2 + 1 - me.y), (me.diag, (1 - me.x) * 2 + 1 - me.y))
    ):
        remote(R.bslot.at[j], R.bslot.at[j], R.bc_s.at[i], R.bc_r.at[i], device).start()
        crossing.append(remote(R.bslot.at[k], R.bslot.at[k], R.bc_s.at[i], R.bc_r.at[i], device))
    x_steps[2]()
    dhn.relay()
    for c in crossing:
        c.wait()
    v = R.bslot[0].astype(f32)
    for k in range(1, 4):
        v = v + R.bslot[k].astype(f32)
    R.bfin[me.c] = v.astype(bf16)
    bc_last = remote(R.bfin.at[me.c], R.bfin.at[me.c], R.mate_s.at[2], R.mate_r.at[2], me.mate)
    bc_last.start()
    for d in range(1, n):
        k, device = me.line(d)
        remote(R.sv, R.lslot.at[k], R.ls_s.at[k], R.ls_r.at[k], device).wait()
    total = R.lslot[0]
    for k in range(1, n):
        total = total + R.lslot[k]
    R.pv[...] = total
    for d in range(1, 8):
        k, device = me.plane(d)
        remote(R.pv, R.small.at[me.q], R.ps_s.at[k], R.ps_r.at[me.q], device).start()
    R.small[me.q] = total
    z_sum.total(put(R.gz))
    leaving[1].start()
    dt_sum.total(put(R.gdt_out))
    bc_last.wait_send()
    remote(
        R.bfin.at[1 - me.c], R.bfin.at[1 - me.c], R.mate_s.at[2], R.mate_r.at[2], me.mate
    ).wait_recv()
    R.gbc[:, 0:128] = R.bfin[0].astype(f32)
    R.gbc[:, 128:256] = R.bfin[1].astype(f32)
    leaving[2].start()
    x_sum.total(put(R.gx))
    leaving[3].start()

    cot_again = pltpu.make_async_copy(R.gcot, R.hn.at[0:SPAN, :], R.loc.at[11])
    cot_again.start()

    def put_dh(k, v):
        R.y[0:SPAN, aligned(k * 128, 128)] = v.T

    dhn.total(put_dh)
    cot_again.wait()

    @over(SPAN // 32)
    def _(i):
        some = aligned(i * 32, 32)
        u = R.hid[some, :].astype(f32)
        qn = lax.rsqrt(jnp.mean(u * u, axis=1, keepdims=True) + EPS)
        w = R.y[some, 0:D] * R.gains[...]
        dot = jnp.sum(w * u, axis=1, keepdims=True) / D
        R.hn[aligned(SPAN + i * 32, 32), :] = (
            R.hn[some, :].astype(f32) + qn * w - u * (qn * qn * qn * dot)
        ).astype(bf16)

    in_copy = pltpu.make_async_copy(R.hn.at[SPAN : 2 * SPAN, :], R.out_grad, R.loc.at[7])
    in_copy.start()
    for d in range(1, 8):
        k, device = me.plane(d)
        remote(R.pv, R.small.at[k], R.ps_s.at[k], R.ps_r.at[k], device).wait()
    leaving[4].start()
    leaving[5].start()
    dhn.finish(False)
    for fin in (x_sum, z_sum, bc_sum, dt_sum):
        for s in line(fin.finish):
            s()
    in_copy.wait()
    out_copy.wait()
    for copy in leaving:
        copy.wait()


def unpack(names, C, H, *refs):
    R = types.SimpleNamespace(**dict(zip(names, refs)))
    ins = ("small", "dt", "wo", "z", "x", "bc", "block", "grad")
    come = [pltpu.make_async_copy(getattr(R, "out_" + k), getattr(R, "v_" + k), R.sem.at[i]) for i, k in enumerate(ins)]
    outs = [k for k in names if k.startswith("o_")]
    there = dict(o_z="v_z", o_x="v_x", o_bc="v_bc", o_block="v_block", o_grad="v_grad")
    go = {
        k: pltpu.make_async_copy(getattr(R, there.get(k, "s_" + k)), getattr(R, k), R.sem.at[len(ins) + i])
        for i, k in enumerate(outs)
    }
    for copy in come:
        copy.start()
    come[0].wait()
    row = lambda k: jnp.concatenate([R.v_small[q, k : k + 1, :] for q in range(8)], axis=1)
    for k in range(KERNEL):
        R.s_o_cx[k : k + 1, :] = row(k)
    R.s_o_cxb[...] = row(4).reshape(8 * C)
    R.s_o_gate[...] = row(5).reshape(8 * C)
    for ref, at in ((R.s_o_dtb, 0), (R.s_o_alog, 8), (R.s_o_skip, 16)):
        v = jnp.concatenate([R.v_small[q, 6:7, at : at + H] for q in range(8)], axis=1)
        ref[...] = v.reshape(8 * H)
    total = R.v_small[0, 8:24, :]
    for q in range(1, 8):
        total = total + R.v_small[q, 8:24, :]
    R.s_o_cbc[...] = total[0:KERNEL, 0:BC]
    R.s_o_cbcb[...] = total[4:5, 0:BC].reshape(BC)
    D = R.o_ng.shape[0]
    R.s_o_ng[...] = jnp.concatenate([total[8 + k : 9 + k, :] for k in range(D // C)], axis=1).reshape(D)
    come[1].wait()
    R.s_o_dt[...] = R.v_dt[0:H, :]
    come[2].wait()
    R.s_o_wo[...] = R.v_wo[...].T
    for copy in come[3:]:
        copy.wait()
    for copy in go.values():
        copy.start()
    for copy in go.values():
        copy.wait()


def shards(
    n,
    hidden_in,
    lengths,
    perm,
    norm_gain,
    w_z,
    w_x,
    w_dt,
    w_bc,
    conv_x,
    conv_x_bias,
    conv_bc,
    conv_bc_bias,
    dt_bias,
    a_log,
    skip_d,
    gate_gain,
    w_out,
    grad_out,
):
    rows, D = hidden_in.shape
    T = rows * 8
    DS, C = w_z.shape
    H = w_dt.shape[1]
    inner = gate_gain.shape[0]
    nb = T // SPAN
    wide_rows = 2 * C + BC + 16
    inputs = dict(
        hidden_in=hidden_in,
        gcot=grad_out,
        wz=w_z,
        wx=w_x,
        wbc=w_bc,
        in_w_dt=w_dt.T,
        wo=w_out,
        in_gain=norm_gain,
        in_conv_x=conv_x,
        in_conv_xb=conv_x_bias,
        in_conv_bc=conv_bc,
        in_conv_bcb=conv_bc_bias,
        in_dt_bias=dt_bias,
        in_a_log=a_log,
        in_skip=skip_d,
        in_gate=gate_gain,
        lengths=lengths,
        perm=perm,
    )
    outputs = dict(
        out_block=((rows, D), bf16),
        out_grad=((rows, D), bf16),
        out_dt=((16, DS), f32),
        out_z=((DS, C), f32),
        out_x=((DS, C), f32),
        out_bc=((DS, BC), f32),
        out_wo=((DS, C), f32),
        out_small=((8, 24, C), f32),
    )
    scratch = dict(
        **{k: (inputs["in_" + k].shape, f32) for k in LITTLE},
        hid=((rows, D), bf16),
        wo_own=((C, DS), f32),
        gdt_out=((16, DS), f32),
        gz=((DS, C), f32),
        gx=((DS, C), f32),
        gbc=((DS, BC), f32),
        gwo=((DS, C), f32),
        small=((8, 24, C), f32),
        hn=((T, D), bf16),
        cot=((T, D), bf16),
        wd=((D, 2 * C + BC + 128), bf16),
        wcat=((wide_rows, D), bf16),
        wot=((D, C), bf16),
        wout=((C, D), bf16),
        won=((D, C), bf16),
        wdt=((n, 16, DS), bf16),
        pr=((C + BC + 16, SPAN), f32),
        z=((C, T), bf16),
        xr=((C, T), bf16),
        bcr=((BC, T), bf16),
        ux=((C, T), bf16),
        ubc=((BC, T), bf16),
        dr=((8, T), f32),
        y=((C, T), f32),
        gg=((C, T), bf16),
        dyn=((C, T), bf16),
        dcat=((wide_rows, T), bf16),
        states=((nb, C, STATE), bf16),
        state=((C, STATE), f32),
        gm=((SPAN, SPAN), f32),
        dg=((SPAN, SPAN), f32),
        edy=((C, SPAN), bf16),
        wxd=((C, SPAN), bf16),
        lamb=((C, STATE), bf16),
        tail_x=((C, 128), f32),
        tail_bc=((BC, 128), f32),
        head_x=((3, C, 128), f32),
        head_bc=((3, BC, 128), f32),
        px=((7, C, 128), f32),
        pbc=((5, BC, 128), f32),
        ph=((8, 128), f32),
        row=((1, inner), f32),
        gains=((1, D), f32),
        accx=((7, C, 128), f32),
        accbc=((5, BC, 128), f32),
        acch=((2, 8, SPAN), f32),
        sums=((2, nb, SPAN), f32),
        tot=((2, nb, SPAN), f32),
        sslot=((2, 8, nb, SPAN), f32),
        sb=((2, 2, D // 2, SPAN), bf16),
        rb=((4, 2, D // 2, SPAN), bf16),
        da=((D // 2, SPAN), bf16),
        db=((D // 2, SPAN), bf16),
        fx=((2, D // 2, SPAN), bf16),
        fy=((2, D // 2, SPAN), bf16),
        gdt_all=((16, D), bf16),
        gdt=((n, 16, DS), bf16),
        rdt=((n + 1, 16, DS), bf16),
        bsum=((DS, 128), f32),
        bslot=((4, DS, 128), bf16),
        bfin=((2, DS, 128), bf16),
        ng=((1, D), f32),
        sv=((24, C), f32),
        pv=((24, C), f32),
        lslot=((n, 24, C), f32),
    )
    semaphores = dict(
        ag_s=(2, 13),
        ag_r=(2, 13),
        za_s=(5, 2, n - 1),
        za_r=(5, 2, n - 1),
        zr_s=(5, 2, n - 1),
        zr_r=(5, 2, n - 1),
        rs_s=(2, 10),
        rs_r=(2, 10),
        mate_s=(3,),
        mate_r=(3,),
        sum_s=(2, 8),
        sum_r=(2, 8),
        ls_s=(n,),
        ls_r=(n,),
        ps_s=(8,),
        ps_r=(8,),
        bc_s=(3,),
        bc_r=(3,),
        loc=(22,),
    )
    names = [*inputs, *outputs, *scratch, *semaphores, "free"]
    vmem = pl.BlockSpec(memory_space=pltpu.VMEM)
    hbm = pl.BlockSpec(memory_space=pl.ANY)
    smem = pl.BlockSpec(memory_space=pltpu.SMEM)
    where = {k: hbm for k in ("hidden_in", "gcot", "wz", "wx", "wbc", "wo", *outputs)}
    where.update({"in_" + k: hbm for k in LITTLE})
    where.update(lengths=smem, perm=smem)
    out = pl.pallas_call(
        functools.partial(kernel, names, n, C, H),
        out_shape=[jax.ShapeDtypeStruct(*s) for s in outputs.values()],
        in_specs=[where.get(k, vmem) for k in inputs],
        out_specs=[where.get(k, vmem) for k in outputs],
        scratch_shapes=[pltpu.VMEM(*s) for s in scratch.values()]
        + [pltpu.SemaphoreType.DMA(s) for s in semaphores.values()]
        + [pltpu.SemaphoreType.REGULAR((5,))],
        compiler_params=pltpu.CompilerParams(
            collective_id=0, has_side_effects=True, vmem_limit_bytes=(64 << 20) - (1 << 18)
        ),
    )(*inputs.values())

    results = dict(
        o_block=((rows, D), bf16),
        o_grad=((rows, D), bf16),
        o_ng=((D,), f32),
        o_z=((DS, C), f32),
        o_x=((DS, C), f32),
        o_dt=((H, DS), f32),
        o_bc=((DS, BC), f32),
        o_cx=((KERNEL, inner), f32),
        o_cxb=((inner,), f32),
        o_cbc=((KERNEL, BC), f32),
        o_cbcb=((BC,), f32),
        o_dtb=(dt_bias.shape, f32),
        o_alog=(a_log.shape, f32),
        o_skip=(skip_d.shape, f32),
        o_gate=((inner,), f32),
        o_wo=((C, DS), f32),
    )
    held = {"v_" + k[4:]: v for k, v in outputs.items()}
    held.update({"s_" + k: v for k, v in results.items() if "v_" + k[2:] not in held or k in ("o_dt", "o_wo")})
    made = pl.pallas_call(
        functools.partial(unpack, [*outputs, *results, *held, "sem"], C, H),
        out_shape=[jax.ShapeDtypeStruct(*s) for s in results.values()],
        in_specs=[hbm] * len(outputs),
        out_specs=[hbm] * len(results),
        scratch_shapes=[pltpu.VMEM(*s) for s in held.values()]
        + [pltpu.SemaphoreType.DMA((len(outputs) + len(results),))],
    )(*out)
    return tuple(v.T if k == "o_dt" else v for k, v in zip(results, made))


def solution(mesh):
    assert mesh.shape["row"] == 4 and mesh.shape["col"] == 2
    every = P(("dp", "row", "col"), None)
    weight = P("dp", ("row", "col"))
    out = P(("row", "col"), "dp")
    return jax.shard_map(
        functools.partial(shards, mesh.shape["dp"]),
        mesh=mesh,
        in_specs=(every, P(), P("dp"), P(), weight, weight, weight, P("dp", None))
        + (P(),) * 8
        + (out, every),
        out_specs=(every, every, P(), weight, weight, weight, P("dp", None)) + (P(),) * 8 + (out,),
        check_vma=False,
    )
```
